256 devices in a mesh: chan: 16 (over x, y), tm: 16 (over z, core).
Axes of the slice: x: 4, y: 4, z: 8, core: 2. Of those that a mesh axis runs over, the one named last changes fastest.
Arguments:
- raw_strain: bfloat16 [256, 262144], P('chan', 'tm'), may hold values from -60 to 60
- fir_taps: bfloat16 [8, 128], replicated, may hold values from -0.5 to 0.5
- start_basis: float32 [8, 256, 32], replicated, may hold values from -6 to 6
Outputs:
- denoised: float32 [8, 256, 65536], P(None, 'chan', 'tm')
The draws below stay inside these ranges and needn't reach their ends.
All inputs are finite; a program needn't handle non-finite values.
Results may differ from the reference program's by a relative error of at most 0.0003.
Values may be sent and summed in bfloat16 or wider, within the bound.
No kernel may reach another device: no remote copies, remote signals or barrier semaphores. Data moves between devices by JAX's collectives and lax.ppermute only.
A program may use at most 192 MiB of HBM per device.

```python
import math
import jax
import jax.numpy as jnp
from jax import lax

CH = 256
BANDS = 8
TAPS = 128
RANK = 32
ITERS = 3
SAMPLES = 262144


def draw_raw_strain(key, part):
    key = jax.random.fold_in(key, 7)
    keys = jax.random.split(key, 8)
    wave_count = 24
    steps_t = jnp.arange(SAMPLES, dtype=jnp.int32)[None, :]
    time_float = steps_t.astype(jnp.float32)
    cycles = jax.random.randint(keys[0], (wave_count,), 10, 900)
    amplitude = jnp.exp(jax.random.uniform(keys[1], (wave_count,), minval=math.log(0.05), maxval=0.0))
    phase_shift = jax.random.uniform(keys[2], (wave_count, CH, 1), minval=-math.pi, maxval=math.pi)
    channel_gain = jax.random.uniform(keys[3], (wave_count, CH, 1), minval=0.5, maxval=1.5)
    center = jax.random.uniform(keys[4], (wave_count,)) * SAMPLES
    spread = jax.random.uniform(keys[5], (wave_count,), minval=0.1, maxval=0.4) * SAMPLES
    signal_sum = jnp.zeros((CH, SAMPLES), jnp.float32)
    for number in range(wave_count):
        turn_index = cycles[number] * steps_t % 4096
        angle_now = turn_index.astype(jnp.float32) * (2.0 * math.pi / 4096.0) + phase_shift[number]
        envelope = 0.2 + jnp.exp(-jnp.square((time_float - center[number]) / spread[number]))
        signal_sum = signal_sum + amplitude[number] * channel_gain[number] * envelope * jnp.sin(angle_now)
    noise_part = jnp.clip(jax.random.normal(keys[7], (CH, SAMPLES), jnp.float32), -5.0, 5.0)
    return (signal_sum + noise_part).astype(jnp.bfloat16)


def centred(key, extent, width, limit, kind=jnp.bfloat16):
    array = jax.random.normal(key, extent, jnp.float32) * width
    return jnp.minimum(jnp.maximum(array, -limit), limit).astype(kind)


def setup_inputs(seed: int = 0) -> dict:
    splits = jax.random.split(jax.random.key(seed), 4)
    raw_strain = draw_raw_strain(jax.random.fold_in(splits[3], 71), 0)
    fir_taps = centred(splits[1], (BANDS, TAPS), TAPS ** -0.5, 0.5)
    start_basis = centred(splits[2], (BANDS, CH, RANK), 1.0, 6.0, jnp.float32)
    return dict(raw_strain=raw_strain, fir_taps=fir_taps, start_basis=start_basis)


def refine(gram_matrix, subspace):
    for number in range(ITERS):
        image = jnp.einsum('bij,bjk->bik', gram_matrix, subspace, precision=lax.Precision.HIGHEST)
        compact = jnp.einsum('bik,bil->bkl', image, image, precision=lax.Precision.HIGHEST)
        lower_small = jnp.linalg.cholesky(compact)
        subspace = lax.linalg.triangular_solve(lower_small, image, left_side=False, lower=True, transpose_a=True)
    return subspace

def reference(raw_strain, fir_taps, start_basis):
    signal = raw_strain.astype(jnp.float32)[:, None, :]
    padded = jnp.pad(signal, ((0, 0), (0, 0), (TAPS - 4, 0)))
    kernel = fir_taps.astype(jnp.float32)[:, None, :]
    band_out = lax.conv_general_dilated(padded, kernel, (4,), 'VALID', dimension_numbers=('NCH', 'OIH', 'NCH'), precision=lax.Precision.HIGHEST)
    decimated = jnp.transpose(band_out, (1, 0, 2))
    gram_matrix = jnp.einsum('bct,bdt->bcd', decimated, decimated, precision=lax.Precision.HIGHEST)
    subspace = refine(gram_matrix, start_basis)
    coefficients = jnp.einsum('bck,bct->bkt', subspace, decimated, precision=lax.Precision.HIGHEST)
    return jnp.einsum('bck,bkt->bct', subspace, coefficients, precision=lax.Precision.HIGHEST)
```

```python
import jax
import jax.numpy as jnp
from jax import lax
from jax.experimental import pallas as pl
from jax.experimental.pallas import tpu as pltpu
from jax.sharding import PartitionSpec as P

ITERS = 3
RIM = 128
STEP = 512
WINDOW = STEP + RIM
HIGHEST = lax.Precision.HIGHEST
VMEM_LIMIT = 40 * 1024 * 1024


def swapped(block, axis, distance):
    route = [(i, i ^ distance) for i in range(lax.axis_size(axis))]
    return lax.ppermute(block, axis, route)


def dot_nt(a, b, precision=None):
    return lax.dot_general(
        a, b, (((1,), (1,)), ((), ())), precision=precision, preferred_element_type=jnp.float32
    )


def halves(value):
    high = value.astype(jnp.bfloat16)
    return high, (value - high.astype(jnp.float32)).astype(jnp.bfloat16)


def gram_kernel(x_ref, taps_ref, gram_ref, table_ref):
    taps = taps_ref[0].astype(jnp.float32)
    row = jnp.concatenate([taps, jnp.zeros((1, STEP), jnp.float32)], axis=1)
    table = pltpu.roll(jnp.broadcast_to(row, (128, WINDOW)), 4, 1, stride=4, stride_axis=0)
    table = table.astype(jnp.bfloat16)
    table_ref[0] = table
    pieces = [
        dot_nt(x_ref[:, first : first + WINDOW], table)
        for first in range(0, x_ref.shape[1] - RIM, STEP)
    ]
    high, low = halves(jnp.concatenate(pieces, axis=1))
    gram_ref[0] = dot_nt(high, high) + dot_nt(high, low) + dot_nt(low, high)


def decimated_gram(windows, fir_taps):
    channels, samples = windows.shape
    bands = fir_taps.shape[0]
    return pl.pallas_call(
        gram_kernel,
        grid=(bands,),
        in_specs=[
            pl.BlockSpec((channels, samples), lambda b: (0, 0)),
            pl.BlockSpec((1, 1, RIM), lambda b: (b, 0, 0)),
        ],
        out_specs=[
            pl.BlockSpec((1, channels, channels), lambda b: (b, 0, 0)),
            pl.BlockSpec((1, 128, WINDOW), lambda b: (b, 0, 0)),
        ],
        out_shape=[
            jax.ShapeDtypeStruct((bands, channels, channels), jnp.float32),
            jax.ShapeDtypeStruct((bands, 128, WINDOW), jnp.bfloat16),
        ],
        compiler_params=pltpu.CompilerParams(vmem_limit_bytes=VMEM_LIMIT),
        name="decimated_gram",
    )(windows, fir_taps[:, None, :])


def inverse_cholesky(compact):
    rank = compact.shape[0]
    rows = lax.broadcasted_iota(jnp.int32, (rank, rank), 0)
    columns = lax.broadcasted_iota(jnp.int32, (rank, rank), 1)
    unit = (rows == columns).astype(jnp.float32)
    both = jnp.concatenate([compact, unit], axis=1)
    below = lax.broadcasted_iota(jnp.int32, (rank, 1), 0)
    for j in range(rank - 1):
        factor = jnp.where(below > j, both[:, j : j + 1], 0.0) / both[j : j + 1, j : j + 1]
        both = both - factor * both[j : j + 1, :]
    pivots = jnp.sum(unit * both[:, :rank], axis=1, keepdims=True)
    return both[:, rank:] / jnp.sqrt(pivots)


def refine_kernel(half_ref, gram_ref, start_ref, out_ref, basis_ref):
    basis = start_ref[...]
    for _ in range(ITERS):
        image = jnp.dot(gram_ref[...], basis, precision=HIGHEST, preferred_element_type=jnp.float32)
        compact = lax.dot_general(
            image,
            image,
            (((0,), (0,)), ((), ())),
            precision=HIGHEST,
            preferred_element_type=jnp.float32,
        )
        basis = dot_nt(image, inverse_cholesky(compact), HIGHEST)
    basis_ref[...] = basis
    count = out_ref.shape[1]
    part = basis_ref[pl.ds(pl.multiple_of(half_ref[0] * count, count), count), :]
    out_ref[...] = dot_nt(basis, part, HIGHEST)


def projector_half(half, gram_matrix, start):
    channels = gram_matrix.shape[0]
    return pl.pallas_call(
        refine_kernel,
        in_specs=[
            pl.BlockSpec(memory_space=pltpu.SMEM),
            pl.BlockSpec(memory_space=pltpu.VMEM),
            pl.BlockSpec(memory_space=pltpu.VMEM),
        ],
        out_specs=pl.BlockSpec(memory_space=pltpu.VMEM),
        out_shape=jax.ShapeDtypeStruct((channels, channels // 2), jnp.float32),
        scratch_shapes=[pltpu.VMEM(start.shape, jnp.float32)],
        compiler_params=pltpu.CompilerParams(vmem_limit_bytes=VMEM_LIMIT),
        name="projector_half",
    )(half.reshape(1), gram_matrix, start)


def denoise_kernel(x_ref, rim_ref, projector_ref, table_ref, out_ref, mixed_ref):
    bands, own, count = out_ref.shape
    sources, _, samples = x_ref.shape
    rows = bands * own
    projector = jnp.concatenate(
        [
            jnp.concatenate([projector_ref[2 * b], projector_ref[2 * b + 1]], axis=1)
            for b in range(bands)
        ],
        axis=0,
    )
    stacked = jnp.concatenate(halves(projector), axis=0)

    def mix(x, first):
        both = jnp.dot(stacked, x, preferred_element_type=jnp.float32)
        high, low = halves(both[:rows] + both[rows:])
        mixed_ref[:rows, first : first + x.shape[1]] = high
        mixed_ref[rows:, first : first + x.shape[1]] = low

    for first in range(0, samples, STEP):
        mix(x_ref[:, :, first : first + STEP].reshape(sources * own, STEP), first)
    mix(rim_ref[...].reshape(sources * own, RIM), samples)
    blocks = count // 128
    for b in range(bands):
        windows = [
            mixed_ref[part + b * own : part + (b + 1) * own, STEP * m : STEP * m + WINDOW]
            for part in (0, rows)
            for m in range(blocks)
        ]
        both = dot_nt(jnp.concatenate(windows, axis=0), table_ref[b])
        result = both[: blocks * own] + both[blocks * own :]
        for m in range(blocks):
            out_ref[b, :, 128 * m : 128 * m + 128] = result[m * own : (m + 1) * own]


def denoise(gathered, projector, table):
    sources, own, extended = gathered.shape
    bands = table.shape[0]
    samples = 4096
    steps = (extended - RIM) // samples
    return pl.pallas_call(
        denoise_kernel,
        grid=(steps,),
        in_specs=[
            pl.BlockSpec((sources, own, samples), lambda i: (0, 0, i)),
            pl.BlockSpec((sources, own, RIM), lambda i: (0, 0, (i + 1) * (samples // RIM))),
            pl.BlockSpec(projector.shape, lambda i: (0, 0, 0)),
            pl.BlockSpec(table.shape, lambda i: (0, 0, 0)),
        ],
        out_specs=pl.BlockSpec((bands, own, samples // 4), lambda i: (0, 0, i)),
        out_shape=jax.ShapeDtypeStruct((bands, own, steps * samples // 4), jnp.float32),
        scratch_shapes=[pltpu.VMEM((2 * bands * own, samples + RIM), jnp.bfloat16)],
        compiler_params=pltpu.CompilerParams(vmem_limit_bytes=VMEM_LIMIT),
        name="denoise",
    )(gathered, gathered, projector, table)


def shards(raw_strain, fir_taps, start_basis):
    own, samples = raw_strain.shape
    bands = fir_taps.shape[0]
    chan_count, tm_count = lax.axis_size("chan"), lax.axis_size("tm")
    channels = own * chan_count
    place, core = lax.axis_index("chan"), lax.axis_index("tm") % 2
    rim_piece = raw_strain[:, samples - RIM :]
    before = lax.ppermute(rim_piece, "tm", [(i, i + 1) for i in range(tm_count - 1)])
    extended = jnp.concatenate([before, raw_strain], axis=1)
    gathered = lax.all_gather(extended, "chan", axis=0)

    part = samples // chan_count
    windows = jnp.stack(
        [extended[:, part * i : part * i + part + RIM] for i in range(chan_count)], axis=0
    )
    windows = lax.all_to_all(windows, "chan", 0, 0, tiled=True)
    local_gram, table = decimated_gram(windows.reshape(channels, part + RIM), fir_taps)

    local_gram = local_gram.reshape(bands, 2, channels // 2, channels)
    sent = swapped(lax.dynamic_index_in_dim(local_gram, 1 - core, 1, False), "tm", 1)
    summed = lax.dynamic_index_in_dim(local_gram, core, 1, False) + sent
    quarters = summed.reshape(chan_count, channels // 4, channels)
    quarter = jnp.sum(lax.all_to_all(quarters, "chan", 0, 0, tiled=True), axis=0)
    distance = 2
    while distance < tm_count:
        quarter = quarter + swapped(quarter, "tm", distance)
        distance *= 2

    other = swapped(quarter, "tm", 1)
    pair = jnp.where(core == 0, jnp.stack([quarter, other]), jnp.stack([other, quarter]))
    other = swapped(pair, "chan", 1)
    half = place % 2
    four = jnp.where(half == 0, jnp.stack([pair, other], 1), jnp.stack([other, pair], 1))
    start = lax.dynamic_index_in_dim(start_basis, place // 2, 0, False)
    projector = projector_half(half, four.reshape(channels, channels), start)

    projector = projector.reshape(chan_count, own, channels // 2)
    projector = lax.all_to_all(projector, "chan", 0, 0, tiled=True)
    return denoise(gathered, projector, table)


def solution(mesh):
    placed = (P("chan", "tm"), P(), P())
    return jax.shard_map(
        shards, mesh=mesh, in_specs=placed, out_specs=P(None, "chan", "tm"), check_vma=False
    )
```

```python
import jax
import jax.numpy as jnp
from jax import lax
from jax.experimental import pallas as pl
from jax.experimental.pallas import tpu as pltpu
from jax.sharding import PartitionSpec as P

ITERS = 3
RIM = 128
STEP = 512
WINDOW = STEP + RIM
HIGHEST = lax.Precision.HIGHEST
VMEM_LIMIT = 40 * 1024 * 1024


def swapped(block, axis, distance):
    route = [(i, i ^ distance) for i in range(lax.axis_size(axis))]
    return lax.ppermute(block, axis, route)


def dot_nt(a, b, precision=None):
    return lax.dot_general(
        a, b, (((1,), (1,)), ((), ())), precision=precision, preferred_element_type=jnp.float32
    )


def halves(value):
    high = value.astype(jnp.bfloat16)
    return high, (value - high.astype(jnp.float32)).astype(jnp.bfloat16)


def windows_kernel(raw_ref, before_ref, extended_ref, windows_ref):
    count, _, width = windows_ref.shape
    part = width - RIM
    extended_ref[:, :RIM] = before_ref[...]
    extended_ref[:, RIM:] = raw_ref[...]
    for i in range(count):
        first = i * part - RIM
        if i:
            windows_ref[i] = raw_ref[:, first : first + width]
        else:
            windows_ref[i, :, :RIM] = before_ref[...]
            windows_ref[i, :, RIM:] = raw_ref[:, :part]


def overlapping(raw_strain, before, count):
    own, samples = raw_strain.shape
    return pl.pallas_call(
        windows_kernel,
        out_shape=[
            jax.ShapeDtypeStruct((own, samples + RIM), raw_strain.dtype),
            jax.ShapeDtypeStruct((count, own, samples // count + RIM), raw_strain.dtype),
        ],
        compiler_params=pltpu.CompilerParams(vmem_limit_bytes=16 * 1024 * 1024),
        name="overlapping",
    )(raw_strain, before)


def table_kernel(taps_ref, table_ref):
    for b in range(taps_ref.shape[0]):
        row = jnp.concatenate(
            [taps_ref[b].astype(jnp.float32), jnp.zeros((1, STEP), jnp.float32)], axis=1
        )
        table = pltpu.roll(jnp.broadcast_to(row, (128, WINDOW)), 4, 1, stride=4, stride_axis=0)
        table_ref[128 * b : 128 * b + 128, :] = table.astype(table_ref.dtype)


def filter_table(fir_taps):
    return pl.pallas_call(
        table_kernel,
        out_shape=jax.ShapeDtypeStruct((128 * fir_taps.shape[0], WINDOW), fir_taps.dtype),
        compiler_params=pltpu.CompilerParams(vmem_limit_bytes=16 * 1024 * 1024),
        name="filter_table",
    )(fir_taps[:, None, :])


def gram_kernel(core_ref, x_ref, table_ref, kept_ref, sent_ref, packed_ref):
    core = core_ref[0]
    count = packed_ref.shape[0] // 2
    lanes = lax.broadcasted_iota(jnp.int32, (64, 128), 1)
    pieces = [
        dot_nt(x_ref[:, first : first + WINDOW], table_ref[...])
        for first in range(0, x_ref.shape[1] - RIM, STEP)
    ]
    for b in range(kept_ref.shape[0]):
        decimated = jnp.concatenate([p[:, 128 * b : 128 * b + 128] for p in pieces], axis=1)
        high, low = halves(decimated)
        gram = dot_nt(high, high) + dot_nt(high, low) + dot_nt(low, high)
        packed_ref[0:64, :] = gram[0:64, 0:128]
        packed_ref[64:128, :] = gram[0:64, 128:256]
        packed_ref[128:192, :] = gram[64:128, 128:256]
        packed_ref[192:256, :] = gram[128:192, 128:256]
        last = pltpu.roll(gram[192:256, 128:256], 64, 1)
        packed_ref[256:320, :] = jnp.where(lanes < 64, last, gram[64:128, 0:128])
        kept_ref[b] = packed_ref[pl.ds(pl.multiple_of(core * count, 8), count), :]
        sent_ref[b] = packed_ref[pl.ds(pl.multiple_of((1 - core) * count, 8), count), :]


def unpacked(packed):
    first, corner = packed[0:64], packed[256:320]
    upper = jnp.concatenate(
        [first, jnp.concatenate([first.T[64:128], corner[:, 64:128]], axis=1)], axis=0
    )
    third = packed[192:256]
    lower = jnp.concatenate(
        [third, jnp.concatenate([third.T[64:128], corner[:, 0:64]], axis=1)], axis=0
    )
    across = packed[64:192]
    return jnp.concatenate(
        [
            jnp.concatenate([upper, across], axis=1),
            jnp.concatenate([across.T, lower], axis=1),
        ],
        axis=0,
    )


def decimated_gram(core, windows, table):
    channels, samples = windows.shape
    bands = table.shape[0] // 128
    half = jax.ShapeDtypeStruct((bands, 160, 128), jnp.float32)
    half_spec = pl.BlockSpec((2, 160, 128), lambda b: (b, 0, 0))
    return pl.pallas_call(
        gram_kernel,
        grid=(bands // 2,),
        in_specs=[
            pl.BlockSpec(memory_space=pltpu.SMEM),
            pl.BlockSpec((channels, samples), lambda b: (0, 0)),
            pl.BlockSpec((256, WINDOW), lambda b: (b, 0)),
        ],
        out_specs=[half_spec, half_spec],
        out_shape=[half, half],
        scratch_shapes=[pltpu.VMEM((320, 128), jnp.float32)],
        compiler_params=pltpu.CompilerParams(vmem_limit_bytes=VMEM_LIMIT),
        name="decimated_gram",
    )(core.reshape(1), windows, table)


def inverse_cholesky(compact):
    rank = compact.shape[0]
    rows = lax.broadcasted_iota(jnp.int32, (rank, rank), 0)
    columns = lax.broadcasted_iota(jnp.int32, (rank, rank), 1)
    unit = (rows == columns).astype(jnp.float32)
    both = jnp.concatenate([compact, unit], axis=1)
    below = lax.broadcasted_iota(jnp.int32, both.shape, 0)
    for block in range(0, rank, 8):
        spread = [
            jnp.broadcast_to(both[:, block + p : block + p + 1], both.shape) for p in range(8)
        ]
        for p in range(8):
            j = block + p
            column = spread[p]
            factor = jnp.where(below > j, column * (1.0 / column[j : j + 1, :]), 0.0)
            both = both - factor * both[j : j + 1, :]
            for q in range(p + 1, 8):
                spread[q] = spread[q] - factor * spread[q][j : j + 1, :]
    pivots = jnp.sum(unit * both[:, :rank], axis=1, keepdims=True)
    return both[:, rank:] / jnp.sqrt(pivots)


def refine_kernel(
    place_ref, mine_ref, core_ref, chan_ref, both_ref, start_ref, out_ref, gram_ref, basis_ref
):
    core, half = place_ref[0], place_ref[1]
    near = jnp.where(core == 0, mine_ref[...], core_ref[...])
    near_next = jnp.where(core == 0, core_ref[...], mine_ref[...])
    far = jnp.where(core == 0, chan_ref[...], both_ref[...])
    far_next = jnp.where(core == 0, both_ref[...], chan_ref[...])
    packed = jnp.concatenate(
        [
            jnp.where(half == 0, near, far),
            jnp.where(half == 0, far, near),
            jnp.where(half == 0, near_next, far_next),
            jnp.where(half == 0, far_next, near_next),
        ],
        axis=0,
    )
    gram_ref[...] = unpacked(packed)
    basis = start_ref[...]
    for _ in range(ITERS):
        image = jnp.dot(gram_ref[...], basis, precision=HIGHEST, preferred_element_type=jnp.float32)
        compact = lax.dot_general(
            image,
            image,
            (((0,), (0,)), ((), ())),
            precision=HIGHEST,
            preferred_element_type=jnp.float32,
        )
        basis = dot_nt(image, inverse_cholesky(compact), HIGHEST)
    basis_ref[...] = basis
    count = out_ref.shape[1]
    part = basis_ref[pl.ds(pl.multiple_of(half * count, count), count), :]
    out_ref[...] = dot_nt(basis, part, HIGHEST)


def projector_half(place, quarters, start):
    channels = start.shape[0]
    return pl.pallas_call(
        refine_kernel,
        in_specs=[pl.BlockSpec(memory_space=pltpu.SMEM)]
        + [pl.BlockSpec(memory_space=pltpu.VMEM)] * 5,
        out_specs=pl.BlockSpec(memory_space=pltpu.VMEM),
        out_shape=jax.ShapeDtypeStruct((channels, channels // 2), jnp.float32),
        scratch_shapes=[
            pltpu.VMEM((channels, channels), jnp.float32),
            pltpu.VMEM(start.shape, jnp.float32),
        ],
        compiler_params=pltpu.CompilerParams(vmem_limit_bytes=16 * 1024 * 1024),
        name="projector_half",
    )(place, *quarters, start)


def denoise_kernel(x_ref, rim_ref, projector_ref, table_ref, out_ref, mixed_ref):
    bands, own, count = out_ref.shape
    sources, _, samples = x_ref.shape
    rows = bands * own
    projector = jnp.concatenate(
        [
            jnp.concatenate([projector_ref[2 * b], projector_ref[2 * b + 1]], axis=1)
            for b in range(bands)
        ],
        axis=0,
    )
    stacked = jnp.concatenate(halves(projector), axis=0)

    def mix(x, first):
        both = jnp.dot(stacked, x, preferred_element_type=jnp.float32)
        high, low = halves(both[:rows] + both[rows:])
        mixed_ref[:rows, first : first + x.shape[1]] = high
        mixed_ref[rows:, first : first + x.shape[1]] = low

    for first in range(0, samples, STEP):
        mix(x_ref[:, :, first : first + STEP].reshape(sources * own, STEP), first)
    mix(rim_ref[...].reshape(sources * own, RIM), samples)
    blocks = count // 128
    for b in range(bands):
        windows = [
            mixed_ref[part + b * own : part + (b + 1) * own, STEP * m : STEP * m + WINDOW]
            for part in (0, rows)
            for m in range(blocks)
        ]
        both = dot_nt(jnp.concatenate(windows, axis=0), table_ref[128 * b : 128 * b + 128, :])
        result = both[: blocks * own] + both[blocks * own :]
        for m in range(blocks):
            out_ref[b, :, 128 * m : 128 * m + 128] = result[m * own : (m + 1) * own]


def denoise(gathered, projector, table):
    sources, own, extended = gathered.shape
    bands = table.shape[0] // 128
    samples = 4096
    steps = (extended - RIM) // samples
    return pl.pallas_call(
        denoise_kernel,
        grid=(steps,),
        in_specs=[
            pl.BlockSpec((sources, own, samples), lambda i: (0, 0, i)),
            pl.BlockSpec((sources, own, RIM), lambda i: (0, 0, (i + 1) * (samples // RIM))),
            pl.BlockSpec(projector.shape, lambda i: (0, 0, 0)),
            pl.BlockSpec(table.shape, lambda i: (0, 0)),
        ],
        out_specs=pl.BlockSpec((bands, own, samples // 4), lambda i: (0, 0, i)),
        out_shape=jax.ShapeDtypeStruct((bands, own, steps * samples // 4), jnp.float32),
        scratch_shapes=[pltpu.VMEM((2 * bands * own, samples + RIM), jnp.bfloat16)],
        compiler_params=pltpu.CompilerParams(vmem_limit_bytes=60 * 1024 * 1024),
        name="denoise",
    )(gathered, gathered, projector, table)


def shards(raw_strain, fir_taps, start_basis):
    own, samples = raw_strain.shape
    chan_count, tm_count = lax.axis_size("chan"), lax.axis_size("tm")
    channels = own * chan_count
    place, core = lax.axis_index("chan"), lax.axis_index("tm") % 2
    half = place % 2
    rim_piece = raw_strain[:, samples - RIM :]
    before = lax.ppermute(rim_piece, "tm", [(i, i + 1) for i in range(tm_count - 1)])
    extended, windows = overlapping(raw_strain, before, chan_count)
    gathered = lax.all_gather(extended, "chan", axis=0)

    windows = lax.all_to_all(windows, "chan", 0, 0, tiled=True)
    table = filter_table(fir_taps)
    kept, sent = decimated_gram(core, windows.reshape(channels, -1), table)

    quarters = (kept + swapped(sent, "tm", 1)).reshape(chan_count, 80, 128)
    quarter = jnp.sum(lax.all_to_all(quarters, "chan", 0, 0, tiled=True), axis=0)
    distance = 2
    while distance < tm_count:
        quarter = quarter + swapped(quarter, "tm", distance)
        distance *= 2

    everyone = range(chan_count * tm_count)
    across = [(i, i ^ (tm_count + 1)) for i in everyone]
    four = (
        quarter,
        swapped(quarter, "tm", 1),
        swapped(quarter, "chan", 1),
        lax.ppermute(quarter, ("chan", "tm"), across),
    )
    start = lax.dynamic_index_in_dim(start_basis, place // 2, 0, False)
    projector = projector_half(jnp.stack([core, half]), four, start)

    projector = projector.reshape(chan_count, own, channels // 2)
    projector = lax.all_to_all(projector, "chan", 0, 0, tiled=True)
    return denoise(gathered, projector, table)


def solution(mesh):
    placed = (P("chan", "tm"), P(), P())
    return jax.shard_map(
        shards, mesh=mesh, in_specs=placed, out_specs=P(None, "chan", "tm"), check_vma=False
    )
```

```python
import jax
import jax.numpy as jnp
from jax import lax
from jax.experimental import pallas as pl
from jax.experimental.pallas import tpu as pltpu
from jax.sharding import PartitionSpec as P

ITERS = 3
RIM = 128
STEP = 512
WINDOW = STEP + RIM
HIGHEST = lax.Precision.HIGHEST
VMEM_LIMIT = 40 * 1024 * 1024


def swapped(block, axis, distance):
    route = [(i, i ^ distance) for i in range(lax.axis_size(axis))]
    return lax.ppermute(block, axis, route)


def dot_nt(a, b, precision=None):
    return lax.dot_general(
        a, b, (((1,), (1,)), ((), ())), precision=precision, preferred_element_type=jnp.float32
    )


def halves(value):
    high = value.astype(jnp.bfloat16)
    return high, (value - high.astype(jnp.float32)).astype(jnp.bfloat16)


def windows_kernel(raw_ref, before_ref, windows_ref):
    count, _, width = windows_ref.shape
    part = width - 2 * RIM
    for i in range(count):
        first = i * part - RIM
        if i:
            windows_ref[i, :, : part + RIM] = raw_ref[:, first : first + part + RIM]
        else:
            windows_ref[i, :, :RIM] = before_ref[...]
            windows_ref[i, :, RIM : part + RIM] = raw_ref[:, :part]
        windows_ref[i, :, part + RIM :] = before_ref[...]


def overlapping(raw_strain, before, count):
    own, samples = raw_strain.shape
    return pl.pallas_call(
        windows_kernel,
        out_shape=jax.ShapeDtypeStruct(
            (count, own, samples // count + 2 * RIM), raw_strain.dtype
        ),
        compiler_params=pltpu.CompilerParams(vmem_limit_bytes=16 * 1024 * 1024),
        name="overlapping",
    )(raw_strain, before)


def table_kernel(taps_ref, table_ref):
    for b in range(taps_ref.shape[0]):
        row = jnp.concatenate(
            [taps_ref[b].astype(jnp.float32), jnp.zeros((1, STEP), jnp.float32)], axis=1
        )
        table = pltpu.roll(jnp.broadcast_to(row, (128, WINDOW)), 4, 1, stride=4, stride_axis=0)
        table_ref[128 * b : 128 * b + 128, :] = table.astype(table_ref.dtype)


def filter_table(fir_taps):
    return pl.pallas_call(
        table_kernel,
        out_shape=jax.ShapeDtypeStruct((128 * fir_taps.shape[0], WINDOW), fir_taps.dtype),
        compiler_params=pltpu.CompilerParams(vmem_limit_bytes=16 * 1024 * 1024),
        name="filter_table",
    )(fir_taps[:, None, :])


def gram_kernel(core_ref, x_ref, table_ref, kept_ref, sent_ref, packed_ref):
    core = core_ref[0]
    count = packed_ref.shape[0] // 2
    lanes = lax.broadcasted_iota(jnp.int32, (64, 128), 1)
    pieces = [
        dot_nt(x_ref[:, first : first + WINDOW], table_ref[...])
        for first in range(0, x_ref.shape[1] - 2 * RIM, STEP)
    ]
    for b in range(kept_ref.shape[0]):
        decimated = jnp.concatenate([p[:, 128 * b : 128 * b + 128] for p in pieces], axis=1)
        high, low = halves(decimated)
        gram = dot_nt(high, high) + dot_nt(high, low) + dot_nt(low, high)
        packed_ref[0:64, :] = gram[0:64, 0:128]
        packed_ref[64:128, :] = gram[0:64, 128:256]
        packed_ref[128:192, :] = gram[64:128, 128:256]
        packed_ref[192:256, :] = gram[128:192, 128:256]
        last = pltpu.roll(gram[192:256, 128:256], 64, 1)
        packed_ref[256:320, :] = jnp.where(lanes < 64, last, gram[64:128, 0:128])
        kept_ref[b] = packed_ref[pl.ds(pl.multiple_of(core * count, 8), count), :]
        sent_ref[b] = packed_ref[pl.ds(pl.multiple_of((1 - core) * count, 8), count), :]


def unpacked(packed):
    first, corner = packed[0:64], packed[256:320]
    upper = jnp.concatenate(
        [first, jnp.concatenate([first.T[64:128], corner[:, 64:128]], axis=1)], axis=0
    )
    third = packed[192:256]
    lower = jnp.concatenate(
        [third, jnp.concatenate([third.T[64:128], corner[:, 0:64]], axis=1)], axis=0
    )
    across = packed[64:192]
    return jnp.concatenate(
        [
            jnp.concatenate([upper, across], axis=1),
            jnp.concatenate([across.T, lower], axis=1),
        ],
        axis=0,
    )


def decimated_gram(core, windows, table):
    channels, samples = windows.shape
    bands = table.shape[0] // 128
    half = jax.ShapeDtypeStruct((bands, 160, 128), jnp.float32)
    half_spec = pl.BlockSpec((2, 160, 128), lambda b: (b, 0, 0))
    return pl.pallas_call(
        gram_kernel,
        grid=(bands // 2,),
        in_specs=[
            pl.BlockSpec(memory_space=pltpu.SMEM),
            pl.BlockSpec((channels, samples), lambda b: (0, 0)),
            pl.BlockSpec((256, WINDOW), lambda b: (b, 0)),
        ],
        out_specs=[half_spec, half_spec],
        out_shape=[half, half],
        scratch_shapes=[pltpu.VMEM((320, 128), jnp.float32)],
        compiler_params=pltpu.CompilerParams(vmem_limit_bytes=VMEM_LIMIT),
        name="decimated_gram",
    )(core.reshape(1), windows, table)


def inverse_cholesky(compact):
    rank = compact.shape[0]
    rows = lax.broadcasted_iota(jnp.int32, (rank, rank), 0)
    columns = lax.broadcasted_iota(jnp.int32, (rank, rank), 1)
    unit = (rows == columns).astype(jnp.float32)
    both = jnp.concatenate([compact, unit], axis=1)
    below = lax.broadcasted_iota(jnp.int32, both.shape, 0)
    for block in range(0, rank, 8):
        spread = [
            jnp.broadcast_to(both[:, block + p : block + p + 1], both.shape) for p in range(8)
        ]
        for p in range(8):
            j = block + p
            column = spread[p]
            factor = jnp.where(below > j, column * (1.0 / column[j : j + 1, :]), 0.0)
            both = both - factor * both[j : j + 1, :]
            for q in range(p + 1, 8):
                spread[q] = spread[q] - factor * spread[q][j : j + 1, :]
    pivots = jnp.sum(unit * both[:, :rank], axis=1, keepdims=True)
    return both[:, rank:] / jnp.sqrt(pivots)


def refine_kernel(
    place_ref, mine_ref, core_ref, chan_ref, both_ref, start_ref, out_ref, gram_ref, basis_ref
):
    core, half = place_ref[0], place_ref[1]
    near = jnp.where(core == 0, mine_ref[...], core_ref[...])
    near_next = jnp.where(core == 0, core_ref[...], mine_ref[...])
    far = jnp.where(core == 0, chan_ref[...], both_ref[...])
    far_next = jnp.where(core == 0, both_ref[...], chan_ref[...])
    packed = jnp.concatenate(
        [
            jnp.where(half == 0, near, far),
            jnp.where(half == 0, far, near),
            jnp.where(half == 0, near_next, far_next),
            jnp.where(half == 0, far_next, near_next),
        ],
        axis=0,
    )
    gram_ref[...] = unpacked(packed)
    basis = start_ref[...]
    for _ in range(ITERS):
        image = jnp.dot(gram_ref[...], basis, precision=HIGHEST, preferred_element_type=jnp.float32)
        compact = lax.dot_general(
            image,
            image,
            (((0,), (0,)), ((), ())),
            precision=HIGHEST,
            preferred_element_type=jnp.float32,
        )
        basis = dot_nt(image, inverse_cholesky(compact), HIGHEST)
    basis_ref[...] = basis
    count = out_ref.shape[1]
    part = basis_ref[pl.ds(pl.multiple_of(half * count, count), count), :]
    out_ref[...] = dot_nt(basis, part, HIGHEST)


def projector_half(place, quarters, start):
    channels = start.shape[0]
    return pl.pallas_call(
        refine_kernel,
        in_specs=[pl.BlockSpec(memory_space=pltpu.SMEM)]
        + [pl.BlockSpec(memory_space=pltpu.VMEM)] * 5,
        out_specs=pl.BlockSpec(memory_space=pltpu.VMEM),
        out_shape=jax.ShapeDtypeStruct((channels, channels // 2), jnp.float32),
        scratch_shapes=[
            pltpu.VMEM((channels, channels), jnp.float32),
            pltpu.VMEM(start.shape, jnp.float32),
        ],
        compiler_params=pltpu.CompilerParams(vmem_limit_bytes=16 * 1024 * 1024),
        name="projector_half",
    )(place, *quarters, start)


def denoise_kernel(x_ref, rim_ref, projector_ref, table_ref, out_ref, mixed_ref):
    bands, own, count = out_ref.shape
    sources, _, samples = x_ref.shape
    rows = bands * own
    projector = jnp.concatenate(
        [
            jnp.concatenate([projector_ref[2 * b], projector_ref[2 * b + 1]], axis=1)
            for b in range(bands)
        ],
        axis=0,
    )
    stacked = jnp.concatenate(halves(projector), axis=0)

    def mix(x, first):
        both = jnp.dot(stacked, x, preferred_element_type=jnp.float32)
        high, low = halves(both[:rows] + both[rows:])
        mixed_ref[:rows, first : first + x.shape[1]] = high
        mixed_ref[rows:, first : first + x.shape[1]] = low

    @pl.when(pl.program_id(0) == 0)
    def _():
        mix(rim_ref[...].reshape(sources * own, RIM), 0)

    @pl.when(pl.program_id(0) > 0)
    def _():
        mixed_ref[:, :RIM] = mixed_ref[:, samples:]

    for first in range(0, samples, STEP):
        mix(x_ref[:, :, first : first + STEP].reshape(sources * own, STEP), RIM + first)
    blocks = count // 128
    for b in range(bands):
        windows = [
            mixed_ref[part + b * own : part + (b + 1) * own, STEP * m : STEP * m + WINDOW]
            for part in (0, rows)
            for m in range(blocks)
        ]
        both = dot_nt(jnp.concatenate(windows, axis=0), table_ref[128 * b : 128 * b + 128, :])
        result = both[: blocks * own] + both[blocks * own :]
        for m in range(blocks):
            out_ref[b, :, 128 * m : 128 * m + 128] = result[m * own : (m + 1) * own]


def denoise(gathered, windows, projector, table):
    sources, own, block = gathered.shape
    bands = table.shape[0] // 128
    samples = 4096
    steps = block // samples
    rim_place = windows.shape[2] // RIM - 1
    return pl.pallas_call(
        denoise_kernel,
        grid=(steps,),
        in_specs=[
            pl.BlockSpec((sources, own, samples), lambda i: (0, 0, i)),
            pl.BlockSpec((sources, own, RIM), lambda i: (0, 0, rim_place)),
            pl.BlockSpec(projector.shape, lambda i: (0, 0, 0)),
            pl.BlockSpec(table.shape, lambda i: (0, 0)),
        ],
        out_specs=pl.BlockSpec((bands, own, samples // 4), lambda i: (0, 0, i)),
        out_shape=jax.ShapeDtypeStruct((bands, own, steps * samples // 4), jnp.float32),
        scratch_shapes=[pltpu.VMEM((2 * bands * own, samples + RIM), jnp.bfloat16)],
        compiler_params=pltpu.CompilerParams(vmem_limit_bytes=58 * 1024 * 1024),
        name="denoise",
    )(gathered, windows, projector, table)


def shards(raw_strain, fir_taps, start_basis):
    own, samples = raw_strain.shape
    chan_count, tm_count = lax.axis_size("chan"), lax.axis_size("tm")
    channels = own * chan_count
    place, core = lax.axis_index("chan"), lax.axis_index("tm") % 2
    half = place % 2
    rim_piece = raw_strain[:, samples - RIM :]
    before = lax.ppermute(rim_piece, "tm", [(i, i + 1) for i in range(tm_count - 1)])
    gathered = lax.all_gather(raw_strain, "chan", axis=0)

    windows = overlapping(raw_strain, before, chan_count)
    windows = lax.all_to_all(windows, "chan", 0, 0, tiled=True)
    table = filter_table(fir_taps)
    kept, sent = decimated_gram(core, windows.reshape(channels, -1), table)

    quarters = (kept + swapped(sent, "tm", 1)).reshape(chan_count, 80, 128)
    quarter = jnp.sum(lax.all_to_all(quarters, "chan", 0, 0, tiled=True), axis=0)
    near = [swapped(quarter, "tm", distance) for distance in (2, 4, 6)]
    quarter = (quarter + near[0]) + (near[1] + near[2])
    quarter = quarter + swapped(quarter, "tm", 8)

    everyone = range(chan_count * tm_count)
    across = [(i, i ^ (tm_count + 1)) for i in everyone]
    four = (
        quarter,
        swapped(quarter, "tm", 1),
        swapped(quarter, "chan", 1),
        lax.ppermute(quarter, ("chan", "tm"), across),
    )
    start = lax.dynamic_index_in_dim(start_basis, place // 2, 0, False)
    projector = projector_half(jnp.stack([core, half]), four, start)

    projector = projector.reshape(chan_count, own, channels // 2)
    projector = lax.all_to_all(projector, "chan", 0, 0, tiled=True)
    return denoise(gathered, windows, projector, table)


def solution(mesh):
    placed = (P("chan", "tm"), P(), P())
    return jax.shard_map(
        shards, mesh=mesh, in_specs=placed, out_specs=P(None, "chan", "tm"), check_vma=False
    )
```

```python
import jax
import jax.numpy as jnp
from jax import lax
from jax.experimental import pallas as pl
from jax.experimental.pallas import tpu as pltpu
from jax.sharding import PartitionSpec as P

ITERS = 3
RIM = 128
STEP = 512
WINDOW = STEP + RIM
HIGHEST = lax.Precision.HIGHEST
VMEM_LIMIT = 40 * 1024 * 1024


def swapped(block, axis, distance):
    route = [(i, i ^ distance) for i in range(lax.axis_size(axis))]
    return lax.ppermute(block, axis, route)


def dot_nt(a, b, precision=None):
    return lax.dot_general(
        a, b, (((1,), (1,)), ((), ())), precision=precision, preferred_element_type=jnp.float32
    )


def halves(value):
    high = value.astype(jnp.bfloat16)
    return high, (value - high.astype(jnp.float32)).astype(jnp.bfloat16)


def windows_kernel(raw_ref, before_ref, extended_ref, windows_ref):
    count, _, width = windows_ref.shape
    part = width - RIM
    extended_ref[:, :RIM] = before_ref[...]
    extended_ref[:, RIM:] = raw_ref[...]
    for i in range(count):
        first = i * part - RIM
        if i:
            windows_ref[i] = raw_ref[:, first : first + width]
        else:
            windows_ref[i, :, :RIM] = before_ref[...]
            windows_ref[i, :, RIM:] = raw_ref[:, :part]


def overlapping(raw_strain, before, count):
    own, samples = raw_strain.shape
    return pl.pallas_call(
        windows_kernel,
        out_shape=[
            jax.ShapeDtypeStruct((own, samples + RIM), raw_strain.dtype),
            jax.ShapeDtypeStruct((count, own, samples // count + RIM), raw_strain.dtype),
        ],
        compiler_params=pltpu.CompilerParams(vmem_limit_bytes=60 * 1024 * 1024),
        name="overlapping",
    )(raw_strain, before)


def table_kernel(taps_ref, table_ref):
    for b in range(taps_ref.shape[0]):
        row = jnp.concatenate(
            [taps_ref[b].astype(jnp.float32), jnp.zeros((1, STEP), jnp.float32)], axis=1
        )
        table = pltpu.roll(jnp.broadcast_to(row, (128, WINDOW)), 4, 1, stride=4, stride_axis=0)
        table_ref[128 * b : 128 * b + 128, :] = table.astype(table_ref.dtype)


def filter_table(fir_taps):
    return pl.pallas_call(
        table_kernel,
        out_shape=jax.ShapeDtypeStruct((128 * fir_taps.shape[0], WINDOW), fir_taps.dtype),
        compiler_params=pltpu.CompilerParams(vmem_limit_bytes=16 * 1024 * 1024),
        name="filter_table",
    )(fir_taps[:, None, :])


def gram_kernel(core_ref, x_ref, table_ref, kept_ref, sent_ref, packed_ref):
    core = core_ref[0]
    count = packed_ref.shape[0] // 2
    lanes = lax.broadcasted_iota(jnp.int32, (64, 128), 1)
    pieces = [
        dot_nt(x_ref[:, first : first + WINDOW], table_ref[...])
        for first in range(0, x_ref.shape[1] - RIM, STEP)
    ]
    for b in range(kept_ref.shape[0]):
        decimated = jnp.concatenate([p[:, 128 * b : 128 * b + 128] for p in pieces], axis=1)
        high, low = halves(decimated)
        gram = dot_nt(high, high) + dot_nt(high, low) + dot_nt(low, high)
        packed_ref[0:64, :] = gram[0:64, 0:128]
        packed_ref[64:128, :] = gram[0:64, 128:256]
        packed_ref[128:192, :] = gram[64:128, 128:256]
        packed_ref[192:256, :] = gram[128:192, 128:256]
        last = pltpu.roll(gram[192:256, 128:256], 64, 1)
        packed_ref[256:320, :] = jnp.where(lanes < 64, last, gram[64:128, 0:128])
        kept_ref[b] = packed_ref[pl.ds(pl.multiple_of(core * count, 8), count), :]
        sent_ref[b] = packed_ref[pl.ds(pl.multiple_of((1 - core) * count, 8), count), :]


def unpacked(packed):
    first, corner = packed[0:64], packed[256:320]
    upper = jnp.concatenate(
        [first, jnp.concatenate([first.T[64:128], corner[:, 64:128]], axis=1)], axis=0
    )
    third = packed[192:256]
    lower = jnp.concatenate(
        [third, jnp.concatenate([third.T[64:128], corner[:, 0:64]], axis=1)], axis=0
    )
    across = packed[64:192]
    return jnp.concatenate(
        [
            jnp.concatenate([upper, across], axis=1),
            jnp.concatenate([across.T, lower], axis=1),
        ],
        axis=0,
    )


def decimated_gram(core, windows, table):
    channels, samples = windows.shape
    bands = table.shape[0] // 128
    half = jax.ShapeDtypeStruct((bands, 160, 128), jnp.float32)
    half_spec = pl.BlockSpec((2, 160, 128), lambda b: (b, 0, 0))
    return pl.pallas_call(
        gram_kernel,
        grid=(bands // 2,),
        in_specs=[
            pl.BlockSpec(memory_space=pltpu.SMEM),
            pl.BlockSpec((channels, samples), lambda b: (0, 0)),
            pl.BlockSpec((256, WINDOW), lambda b: (b, 0)),
        ],
        out_specs=[half_spec, half_spec],
        out_shape=[half, half],
        scratch_shapes=[pltpu.VMEM((320, 128), jnp.float32)],
        compiler_params=pltpu.CompilerParams(vmem_limit_bytes=VMEM_LIMIT),
        name="decimated_gram",
    )(core.reshape(1), windows, table)


def inverse_cholesky(compact):
    rank = compact.shape[0]
    rows = lax.broadcasted_iota(jnp.int32, (rank, rank), 0)
    columns = lax.broadcasted_iota(jnp.int32, (rank, rank), 1)
    unit = (rows == columns).astype(jnp.float32)
    both = jnp.concatenate([compact, unit], axis=1)
    below = lax.broadcasted_iota(jnp.int32, both.shape, 0)
    for block in range(0, rank, 8):
        spread = [
            jnp.broadcast_to(both[:, block + p : block + p + 1], both.shape) for p in range(8)
        ]
        for p in range(8):
            j = block + p
            column = spread[p]
            factor = jnp.where(below > j, column * (1.0 / column[j : j + 1, :]), 0.0)
            both = both - factor * both[j : j + 1, :]
            for q in range(p + 1, 8):
                spread[q] = spread[q] - factor * spread[q][j : j + 1, :]
    pivots = jnp.sum(unit * both[:, :rank], axis=1, keepdims=True)
    return both[:, rank:] / jnp.sqrt(pivots)


def refine_kernel(
    place_ref, mine_ref, core_ref, chan_ref, both_ref, start_ref, out_ref, gram_ref, basis_ref
):
    core, half = place_ref[0], place_ref[1]
    near = jnp.where(core == 0, mine_ref[...], core_ref[...])
    near_next = jnp.where(core == 0, core_ref[...], mine_ref[...])
    far = jnp.where(core == 0, chan_ref[...], both_ref[...])
    far_next = jnp.where(core == 0, both_ref[...], chan_ref[...])
    packed = jnp.concatenate(
        [
            jnp.where(half == 0, near, far),
            jnp.where(half == 0, far, near),
            jnp.where(half == 0, near_next, far_next),
            jnp.where(half == 0, far_next, near_next),
        ],
        axis=0,
    )
    gram_ref[...] = unpacked(packed)
    basis = start_ref[...]
    for _ in range(ITERS):
        image = jnp.dot(gram_ref[...], basis, precision=HIGHEST, preferred_element_type=jnp.float32)
        compact = lax.dot_general(
            image,
            image,
            (((0,), (0,)), ((), ())),
            precision=HIGHEST,
            preferred_element_type=jnp.float32,
        )
        basis = dot_nt(image, inverse_cholesky(compact), HIGHEST)
    basis_ref[...] = basis
    count = out_ref.shape[1]
    part = basis_ref[pl.ds(pl.multiple_of(half * count, count), count), :]
    out_ref[...] = dot_nt(basis, part, HIGHEST)


def projector_half(place, quarters, start):
    channels = start.shape[0]
    return pl.pallas_call(
        refine_kernel,
        in_specs=[pl.BlockSpec(memory_space=pltpu.SMEM)]
        + [pl.BlockSpec(memory_space=pltpu.VMEM)] * 5,
        out_specs=pl.BlockSpec(memory_space=pltpu.VMEM),
        out_shape=jax.ShapeDtypeStruct((channels, channels // 2), jnp.float32),
        scratch_shapes=[
            pltpu.VMEM((channels, channels), jnp.float32),
            pltpu.VMEM(start.shape, jnp.float32),
        ],
        compiler_params=pltpu.CompilerParams(vmem_limit_bytes=16 * 1024 * 1024),
        name="projector_half",
    )(place, *quarters, start)


def denoise_kernel(x_ref, rim_ref, projector_ref, table_ref, out_ref, mixed_ref):
    bands, own, count = out_ref.shape
    sources, _, samples = x_ref.shape
    rows = bands * own
    projector = jnp.concatenate(
        [
            jnp.concatenate([projector_ref[2 * b], projector_ref[2 * b + 1]], axis=1)
            for b in range(bands)
        ],
        axis=0,
    )
    stacked = jnp.concatenate(halves(projector), axis=0)

    def mix(x, first):
        both = jnp.dot(stacked, x, preferred_element_type=jnp.float32)
        high, low = halves(both[:rows] + both[rows:])
        mixed_ref[:rows, first : first + x.shape[1]] = high
        mixed_ref[rows:, first : first + x.shape[1]] = low

    for first in range(0, samples, STEP):
        mix(x_ref[:, :, first : first + STEP].reshape(sources * own, STEP), first)
    mix(rim_ref[...].reshape(sources * own, RIM), samples)
    blocks = count // 128
    for b in range(bands):
        windows = [
            mixed_ref[part + b * own : part + (b + 1) * own, STEP * m : STEP * m + WINDOW]
            for part in (0, rows)
            for m in range(blocks)
        ]
        both = dot_nt(jnp.concatenate(windows, axis=0), table_ref[128 * b : 128 * b + 128, :])
        result = both[: blocks * own] + both[blocks * own :]
        for m in range(blocks):
            out_ref[b, :, 128 * m : 128 * m + 128] = result[m * own : (m + 1) * own]


def denoise(gathered, projector, table):
    sources, own, extended = gathered.shape
    bands = table.shape[0] // 128
    samples = 4096
    steps = (extended - RIM) // samples
    return pl.pallas_call(
        denoise_kernel,
        grid=(steps,),
        in_specs=[
            pl.BlockSpec((sources, own, samples), lambda i: (0, 0, i)),
            pl.BlockSpec((sources, own, RIM), lambda i: (0, 0, (i + 1) * (samples // RIM))),
            pl.BlockSpec(projector.shape, lambda i: (0, 0, 0)),
            pl.BlockSpec(table.shape, lambda i: (0, 0)),
        ],
        out_specs=pl.BlockSpec((bands, own, samples // 4), lambda i: (0, 0, i)),
        out_shape=jax.ShapeDtypeStruct((bands, own, steps * samples // 4), jnp.float32),
        scratch_shapes=[pltpu.VMEM((2 * bands * own, samples + RIM), jnp.bfloat16)],
        compiler_params=pltpu.CompilerParams(vmem_limit_bytes=58 * 1024 * 1024),
        name="denoise",
    )(gathered, gathered, projector, table)


def shards(raw_strain, fir_taps, start_basis):
    own, samples = raw_strain.shape
    chan_count, tm_count = lax.axis_size("chan"), lax.axis_size("tm")
    channels = own * chan_count
    place, core = lax.axis_index("chan"), lax.axis_index("tm") % 2
    half = place % 2
    rim_piece = raw_strain[:, samples - RIM :]
    before = lax.ppermute(rim_piece, "tm", [(i, i + 1) for i in range(tm_count - 1)])
    extended, windows = overlapping(raw_strain, before, chan_count)
    gathered = lax.all_gather(extended, "chan", axis=0)

    windows = lax.all_to_all(windows, "chan", 0, 0, tiled=True)
    table = filter_table(fir_taps)
    kept, sent = decimated_gram(core, windows.reshape(channels, -1), table)

    quarters = (kept + swapped(sent, "tm", 1)).reshape(chan_count, 80, 128)
    quarter = jnp.sum(lax.all_to_all(quarters, "chan", 0, 0, tiled=True), axis=0)
    quarter = quarter + swapped(quarter, "tm", 2)
    others = [swapped(quarter, "tm", distance) for distance in (4, 8, 12)]
    quarter = (quarter + others[0]) + (others[1] + others[2])

    everyone = range(chan_count * tm_count)
    across = [(i, i ^ (tm_count + 1)) for i in everyone]
    four = (
        quarter,
        swapped(quarter, "tm", 1),
        swapped(quarter, "chan", 1),
        lax.ppermute(quarter, ("chan", "tm"), across),
    )
    start = lax.dynamic_index_in_dim(start_basis, place // 2, 0, False)
    projector = projector_half(jnp.stack([core, half]), four, start)

    projector = projector.reshape(chan_count, own, channels // 2)
    projector = lax.all_to_all(projector, "chan", 0, 0, tiled=True)
    return denoise(gathered, projector, table)


def solution(mesh):
    placed = (P("chan", "tm"), P(), P())
    return jax.shard_map(
        shards, mesh=mesh, in_specs=placed, out_specs=P(None, "chan", "tm"), check_vma=False
    )
```

```python
import jax
import jax.numpy as jnp
from jax import lax
from jax.experimental import pallas as pl
from jax.experimental.pallas import tpu as pltpu
from jax.sharding import PartitionSpec as P

ITERS = 3
RIM = 128
STEP = 512
WINDOW = STEP + RIM
HIGHEST = lax.Precision.HIGHEST
VMEM_LIMIT = 24 * 1024 * 1024


def swapped(block, axis, distance):
    route = [(i, i ^ distance) for i in range(lax.axis_size(axis))]
    return lax.ppermute(block, axis, route)


def dot_nt(a, b, precision=None):
    return lax.dot_general(
        a, b, (((1,), (1,)), ((), ())), precision=precision, preferred_element_type=jnp.float32
    )


def halves(value):
    high = value.astype(jnp.bfloat16)
    return high, (value - high.astype(jnp.float32)).astype(jnp.bfloat16)


def windows_kernel(raw_ref, before_ref, windows_ref):
    count, _, width = windows_ref.shape
    part = width - RIM
    for i in range(count):
        first = i * part - RIM
        if i:
            windows_ref[i] = raw_ref[:, first : first + width]
        else:
            windows_ref[i, :, :RIM] = before_ref[...]
            windows_ref[i, :, RIM:] = raw_ref[:, :part]


def overlapping(raw_strain, before, count):
    own, samples = raw_strain.shape
    return pl.pallas_call(
        windows_kernel,
        out_shape=jax.ShapeDtypeStruct((count, own, samples // count + RIM), raw_strain.dtype),
        compiler_params=pltpu.CompilerParams(vmem_limit_bytes=16 * 1024 * 1024),
        name="overlapping",
    )(raw_strain, before)


def table_kernel(taps_ref, table_ref):
    for b in range(taps_ref.shape[0]):
        row = jnp.concatenate(
            [taps_ref[b].astype(jnp.float32), jnp.zeros((1, STEP), jnp.float32)], axis=1
        )
        table = pltpu.roll(jnp.broadcast_to(row, (128, WINDOW)), 4, 1, stride=4, stride_axis=0)
        table_ref[128 * b : 128 * b + 128, :] = table.astype(table_ref.dtype)


def filter_table(fir_taps):
    return pl.pallas_call(
        table_kernel,
        out_shape=jax.ShapeDtypeStruct((128 * fir_taps.shape[0], WINDOW), fir_taps.dtype),
        compiler_params=pltpu.CompilerParams(vmem_limit_bytes=16 * 1024 * 1024),
        name="filter_table",
    )(fir_taps[:, None, :])


def gram_kernel(core_ref, x_ref, table_ref, kept_ref, sent_ref, high_ref, low_ref, packed_ref):
    core = core_ref[0]
    count = packed_ref.shape[0] // 2
    lanes = lax.broadcasted_iota(jnp.int32, (64, 128), 1)
    pieces = [
        dot_nt(x_ref[:, first : first + WINDOW], table_ref[...])
        for first in range(0, x_ref.shape[1] - RIM, STEP)
    ]
    for b in range(kept_ref.shape[0]):
        decimated = jnp.concatenate([p[:, 128 * b : 128 * b + 128] for p in pieces], axis=1)
        high, low = halves(decimated)
        high_ref[b], low_ref[b] = high, low
        gram = dot_nt(high, high) + dot_nt(high, low) + dot_nt(low, high)
        packed_ref[0:64, :] = gram[0:64, 0:128]
        packed_ref[64:128, :] = gram[0:64, 128:256]
        packed_ref[128:192, :] = gram[64:128, 128:256]
        packed_ref[192:256, :] = gram[128:192, 128:256]
        last = pltpu.roll(gram[192:256, 128:256], 64, 1)
        packed_ref[256:320, :] = jnp.where(lanes < 64, last, gram[64:128, 0:128])
        kept_ref[b] = packed_ref[pl.ds(pl.multiple_of(core * count, 8), count), :]
        sent_ref[b] = packed_ref[pl.ds(pl.multiple_of((1 - core) * count, 8), count), :]


def unpacked(packed):
    first, corner = packed[0:64], packed[256:320]
    upper = jnp.concatenate(
        [first, jnp.concatenate([first.T[64:128], corner[:, 64:128]], axis=1)], axis=0
    )
    third = packed[192:256]
    lower = jnp.concatenate(
        [third, jnp.concatenate([third.T[64:128], corner[:, 0:64]], axis=1)], axis=0
    )
    across = packed[64:192]
    return jnp.concatenate(
        [
            jnp.concatenate([upper, across], axis=1),
            jnp.concatenate([across.T, lower], axis=1),
        ],
        axis=0,
    )


def decimated_gram(core, windows, table):
    channels, samples = windows.shape
    bands = table.shape[0] // 128
    half = jax.ShapeDtypeStruct((bands, 160, 128), jnp.float32)
    half_spec = pl.BlockSpec((2, 160, 128), lambda b: (b, 0, 0))
    count = (samples - RIM) // 4
    piece = jax.ShapeDtypeStruct((bands, channels, count), jnp.bfloat16)
    piece_spec = pl.BlockSpec((2, channels, count), lambda b: (b, 0, 0))
    return pl.pallas_call(
        gram_kernel,
        grid=(bands // 2,),
        in_specs=[
            pl.BlockSpec(memory_space=pltpu.SMEM),
            pl.BlockSpec((channels, samples), lambda b: (0, 0)),
            pl.BlockSpec((256, WINDOW), lambda b: (b, 0)),
        ],
        out_specs=[half_spec, half_spec, piece_spec, piece_spec],
        out_shape=[half, half, piece, piece],
        scratch_shapes=[pltpu.VMEM((320, 128), jnp.float32)],
        compiler_params=pltpu.CompilerParams(vmem_limit_bytes=VMEM_LIMIT),
        name="decimated_gram",
    )(core.reshape(1), windows, table)


def inverse_cholesky(compact):
    rank = compact.shape[0]
    rows = lax.broadcasted_iota(jnp.int32, (rank, rank), 0)
    columns = lax.broadcasted_iota(jnp.int32, (rank, rank), 1)
    unit = (rows == columns).astype(jnp.float32)
    both = jnp.concatenate([compact, unit], axis=1)
    below = lax.broadcasted_iota(jnp.int32, both.shape, 0)
    for block in range(0, rank, 8):
        spread = [
            jnp.broadcast_to(both[:, block + p : block + p + 1], both.shape) for p in range(8)
        ]
        for p in range(8):
            j = block + p
            column = spread[p]
            factor = jnp.where(below > j, column * (1.0 / column[j : j + 1, :]), 0.0)
            both = both - factor * both[j : j + 1, :]
            for q in range(p + 1, 8):
                spread[q] = spread[q] - factor * spread[q][j : j + 1, :]
    pivots = jnp.sum(unit * both[:, :rank], axis=1, keepdims=True)
    return both[:, rank:] / jnp.sqrt(pivots)


def refine_kernel(
    place_ref, mine_ref, core_ref, chan_ref, both_ref, start_ref, out_ref, gram_ref, basis_ref
):
    core, half = place_ref[0], place_ref[1]
    near = jnp.where(core == 0, mine_ref[...], core_ref[...])
    near_next = jnp.where(core == 0, core_ref[...], mine_ref[...])
    far = jnp.where(core == 0, chan_ref[...], both_ref[...])
    far_next = jnp.where(core == 0, both_ref[...], chan_ref[...])
    packed = jnp.concatenate(
        [
            jnp.where(half == 0, near, far),
            jnp.where(half == 0, far, near),
            jnp.where(half == 0, near_next, far_next),
            jnp.where(half == 0, far_next, near_next),
        ],
        axis=0,
    )
    gram_ref[...] = unpacked(packed)
    basis = start_ref[...]
    for _ in range(ITERS):
        image = jnp.dot(gram_ref[...], basis, precision=HIGHEST, preferred_element_type=jnp.float32)
        compact = lax.dot_general(
            image,
            image,
            (((0,), (0,)), ((), ())),
            precision=HIGHEST,
            preferred_element_type=jnp.float32,
        )
        basis = dot_nt(image, inverse_cholesky(compact), HIGHEST)
    basis_ref[...] = basis
    rows = lax.broadcasted_iota(jnp.int32, gram_ref.shape, 0)
    columns = lax.broadcasted_iota(jnp.int32, gram_ref.shape, 1)
    trace = jnp.sum(jnp.where(rows == columns, gram_ref[...], 0.0), keepdims=True)
    unit = jnp.sqrt(trace) * 2.0**-15
    count = out_ref.shape[2]
    part = basis_ref[pl.ds(pl.multiple_of(half * count, count), count), :].T
    rank = part.shape[0]
    for i in range(out_ref.shape[0]):
        out_ref[i, :rank] = part
        out_ref[i, rank:] = jnp.broadcast_to(unit, (8, count))


def basis_half(place, quarters, start, receivers):
    channels, rank = start.shape
    return pl.pallas_call(
        refine_kernel,
        in_specs=[pl.BlockSpec(memory_space=pltpu.SMEM)]
        + [pl.BlockSpec(memory_space=pltpu.VMEM)] * 5,
        out_specs=pl.BlockSpec(memory_space=pltpu.VMEM),
        out_shape=jax.ShapeDtypeStruct((receivers, rank + 8, channels // 2), jnp.float32),
        scratch_shapes=[
            pltpu.VMEM((channels, channels), jnp.float32),
            pltpu.VMEM(start.shape, jnp.float32),
        ],
        compiler_params=pltpu.CompilerParams(vmem_limit_bytes=16 * 1024 * 1024),
        name="basis_half",
    )(place, *quarters, start)


def denoise_kernel(basis_ref, high_ref, low_ref, out_ref):
    receivers, bands, own, _ = out_ref.shape
    rank = basis_ref.shape[1] - 8
    for b in range(bands):
        pair = basis_ref[2 * b], basis_ref[2 * b + 1]
        unit = pair[0][rank : rank + 1, 0:1]
        basis = jnp.concatenate([pair[0][:rank], pair[1][:rank]], axis=1)
        basis_high, basis_low = halves(basis)
        both = jnp.dot(
            jnp.concatenate([basis_high, basis_low], axis=0),
            high_ref[b],
            preferred_element_type=jnp.float32,
        )
        coefficients = both[:rank] + both[rank:]
        coefficients += jnp.dot(basis_high, low_ref[b], preferred_element_type=jnp.float32)
        left = jnp.concatenate([basis_high, basis_low, basis_high], axis=0)
        high, low = halves(coefficients * (1.0 / unit))
        result = lax.dot_general(
            left,
            jnp.concatenate([high, high, low], axis=0),
            (((0,), (0,)), ((), ())),
            preferred_element_type=jnp.float32,
        )
        for i in range(receivers):
            out_ref[i, b] = result[i * own : (i + 1) * own]


def denoise(basis, high, low, receivers):
    bands, channels, count = high.shape
    piece_spec = pl.BlockSpec((2, channels, count), lambda b: (b, 0, 0))
    shape = (receivers, bands, channels // receivers, count)
    return pl.pallas_call(
        denoise_kernel,
        grid=(bands // 2,),
        in_specs=[
            pl.BlockSpec((4,) + basis.shape[1:], lambda b: (b, 0, 0)),
            piece_spec,
            piece_spec,
        ],
        out_specs=pl.BlockSpec((receivers, 2) + shape[2:], lambda b: (0, b, 0, 0)),
        out_shape=jax.ShapeDtypeStruct(shape, jnp.float32),
        compiler_params=pltpu.CompilerParams(vmem_limit_bytes=24 * 1024 * 1024),
        name="denoise",
    )(basis, high, low)


def shards(raw_strain, fir_taps, start_basis):
    own, samples = raw_strain.shape
    bands = fir_taps.shape[0]
    chan_count, tm_count = lax.axis_size("chan"), lax.axis_size("tm")
    channels = own * chan_count
    place, core = lax.axis_index("chan"), lax.axis_index("tm") % 2
    half = place % 2
    rim_piece = raw_strain[:, samples - RIM :]
    before = lax.ppermute(rim_piece, "tm", [(i, i + 1) for i in range(tm_count - 1)])

    windows = overlapping(raw_strain, before, chan_count)
    windows = lax.all_to_all(windows, "chan", 0, 0, tiled=True)
    table = filter_table(fir_taps)
    kept, sent, high, low = decimated_gram(core, windows.reshape(channels, -1), table)

    quarters = (kept + swapped(sent, "tm", 1)).reshape(chan_count, 80, 128)
    quarter = jnp.sum(lax.all_to_all(quarters, "chan", 0, 0, tiled=True), axis=0)
    quarter = quarter + swapped(quarter, "tm", 2)
    others = [swapped(quarter, "tm", distance) for distance in (4, 8, 12)]
    quarter = (quarter + others[0]) + (others[1] + others[2])

    everyone = range(chan_count * tm_count)
    across = [(i, i ^ (tm_count + 1)) for i in everyone]
    four = (
        quarter,
        swapped(quarter, "tm", 1),
        swapped(quarter, "chan", 1),
        lax.ppermute(quarter, ("chan", "tm"), across),
    )
    start = lax.dynamic_index_in_dim(start_basis, place // 2, 0, False)
    basis = basis_half(jnp.stack([core, half]), four, start, chan_count)

    basis = lax.all_to_all(basis, "chan", 0, 0, tiled=True)
    units = basis[::2, start.shape[1], 0]
    result = denoise(basis, high, low, chan_count).astype(jnp.float16)
    result = lax.all_to_all(result, "chan", 0, 0, tiled=True)
    result = result.astype(jnp.float32) * units[None, :, None, None]
    return jnp.transpose(result, (1, 2, 0, 3)).reshape(bands, own, samples // 4)


def solution(mesh):
    placed = (P("chan", "tm"), P(), P())
    return jax.shard_map(
        shards, mesh=mesh, in_specs=placed, out_specs=P(None, "chan", "tm"), check_vma=False
    )
```

```python
import jax
import jax.numpy as jnp
from jax import lax
from jax.experimental import pallas as pl
from jax.experimental.pallas import tpu as pltpu
from jax.sharding import PartitionSpec as P

ITERS = 3
RIM = 128
STEP = 512
WINDOW = STEP + RIM
HIGHEST = lax.Precision.HIGHEST
VMEM_LIMIT = 24 * 1024 * 1024


def swapped(block, axis, distance):
    route = [(i, i ^ distance) for i in range(lax.axis_size(axis))]
    return lax.ppermute(block, axis, route)


def dot_nt(a, b, precision=None):
    return lax.dot_general(
        a, b, (((1,), (1,)), ((), ())), precision=precision, preferred_element_type=jnp.float32
    )


def halves(value):
    high = value.astype(jnp.bfloat16)
    return high, (value - high.astype(jnp.float32)).astype(jnp.bfloat16)


def table_kernel(taps_ref, table_ref):
    for b in range(taps_ref.shape[0]):
        row = jnp.concatenate(
            [taps_ref[b].astype(jnp.float32), jnp.zeros((1, STEP), jnp.float32)], axis=1
        )
        table = pltpu.roll(jnp.broadcast_to(row, (128, WINDOW)), 4, 1, stride=4, stride_axis=0)
        table_ref[128 * b : 128 * b + 128, :] = table.astype(table_ref.dtype)


def filter_table(fir_taps):
    return pl.pallas_call(
        table_kernel,
        out_shape=jax.ShapeDtypeStruct((128 * fir_taps.shape[0], WINDOW), fir_taps.dtype),
        compiler_params=pltpu.CompilerParams(vmem_limit_bytes=16 * 1024 * 1024),
        name="filter_table",
    )(fir_taps[:, None, :])


def filter_kernel(raw_ref, before_ref, table_ref, out_ref, extended_ref):
    own, samples = raw_ref.shape
    receivers, _, part = out_ref.shape
    extended_ref[:, :RIM] = before_ref[...]
    extended_ref[:, RIM:] = raw_ref[...]
    blocks = samples // STEP
    windows = jnp.concatenate(
        [extended_ref[:, STEP * m : STEP * m + WINDOW] for m in range(blocks)], axis=0
    )
    bands = table_ref.shape[0] // 128
    share = part // 128
    for pair in range(bands // 2):
        both = dot_nt(windows, table_ref[256 * pair : 256 * pair + 256, :])
        for b in range(2):
            for m in range(blocks):
                place = (2 * pair + b) * (receivers // bands) + m // share
                first = 128 * (m % share)
                out_ref[place, :, first : first + 128] = both[
                    m * own : (m + 1) * own, 128 * b : 128 * b + 128
                ]


def filtered(raw_strain, before, table, receivers):
    own, samples = raw_strain.shape
    part = table.shape[0] // 128 * (samples // 4) // receivers
    return pl.pallas_call(
        filter_kernel,
        out_shape=jax.ShapeDtypeStruct((receivers, own, part), jnp.float32),
        scratch_shapes=[pltpu.VMEM((own, samples + RIM), raw_strain.dtype)],
        compiler_params=pltpu.CompilerParams(vmem_limit_bytes=VMEM_LIMIT),
        name="filtered",
    )(raw_strain, before, table)


def gram_kernel(core_ref, samples_ref, kept_ref, sent_ref, packed_ref):
    core = core_ref[0]
    count = packed_ref.shape[0] // 2
    lanes = lax.broadcasted_iota(jnp.int32, (64, 128), 1)
    high, low = halves(samples_ref[...])
    gram = dot_nt(high, high) + dot_nt(high, low) + dot_nt(low, high)
    packed_ref[0:64, :] = gram[0:64, 0:128]
    packed_ref[64:128, :] = gram[0:64, 128:256]
    packed_ref[128:192, :] = gram[64:128, 128:256]
    packed_ref[192:256, :] = gram[128:192, 128:256]
    last = pltpu.roll(gram[192:256, 128:256], 64, 1)
    packed_ref[256:320, :] = jnp.where(lanes < 64, last, gram[64:128, 0:128])
    kept_ref[...] = packed_ref[pl.ds(pl.multiple_of(core * count, 8), count), :]
    sent_ref[...] = packed_ref[pl.ds(pl.multiple_of((1 - core) * count, 8), count), :]


def band_gram(core, samples):
    half = jax.ShapeDtypeStruct((160, 128), jnp.float32)
    return pl.pallas_call(
        gram_kernel,
        in_specs=[
            pl.BlockSpec(memory_space=pltpu.SMEM),
            pl.BlockSpec(memory_space=pltpu.VMEM),
        ],
        out_shape=[half, half],
        scratch_shapes=[pltpu.VMEM((320, 128), jnp.float32)],
        compiler_params=pltpu.CompilerParams(vmem_limit_bytes=VMEM_LIMIT),
        name="band_gram",
    )(core.reshape(1), samples)


def unpacked(packed):
    first, corner = packed[0:64], packed[256:320]
    upper = jnp.concatenate(
        [first, jnp.concatenate([first.T[64:128], corner[:, 64:128]], axis=1)], axis=0
    )
    third = packed[192:256]
    lower = jnp.concatenate(
        [third, jnp.concatenate([third.T[64:128], corner[:, 0:64]], axis=1)], axis=0
    )
    across = packed[64:192]
    return jnp.concatenate(
        [
            jnp.concatenate([upper, across], axis=1),
            jnp.concatenate([across.T, lower], axis=1),
        ],
        axis=0,
    )


def decimated_gram(core, windows, table):
    channels, samples = windows.shape
    bands = table.shape[0] // 128
    half = jax.ShapeDtypeStruct((bands, 160, 128), jnp.float32)
    half_spec = pl.BlockSpec((2, 160, 128), lambda b: (b, 0, 0))
    count = (samples - RIM) // 4
    piece = jax.ShapeDtypeStruct((bands, channels, count), jnp.bfloat16)
    piece_spec = pl.BlockSpec((2, channels, count), lambda b: (b, 0, 0))
    return pl.pallas_call(
        gram_kernel,
        grid=(bands // 2,),
        in_specs=[
            pl.BlockSpec(memory_space=pltpu.SMEM),
            pl.BlockSpec((channels, samples), lambda b: (0, 0)),
            pl.BlockSpec((256, WINDOW), lambda b: (b, 0)),
        ],
        out_specs=[half_spec, half_spec, piece_spec, piece_spec],
        out_shape=[half, half, piece, piece],
        scratch_shapes=[pltpu.VMEM((320, 128), jnp.float32)],
        compiler_params=pltpu.CompilerParams(vmem_limit_bytes=VMEM_LIMIT),
        name="decimated_gram",
    )(core.reshape(1), windows, table)


def inverse_cholesky(compact):
    rank = compact.shape[0]
    rows = lax.broadcasted_iota(jnp.int32, (rank, rank), 0)
    columns = lax.broadcasted_iota(jnp.int32, (rank, rank), 1)
    unit = (rows == columns).astype(jnp.float32)
    both = jnp.concatenate([compact, unit], axis=1)
    below = lax.broadcasted_iota(jnp.int32, both.shape, 0)
    for block in range(0, rank, 8):
        spread = [
            jnp.broadcast_to(both[:, block + p : block + p + 1], both.shape) for p in range(8)
        ]
        for p in range(8):
            j = block + p
            column = spread[p]
            factor = jnp.where(below > j, column * (1.0 / column[j : j + 1, :]), 0.0)
            both = both - factor * both[j : j + 1, :]
            for q in range(p + 1, 8):
                spread[q] = spread[q] - factor * spread[q][j : j + 1, :]
    pivots = jnp.sum(unit * both[:, :rank], axis=1, keepdims=True)
    return both[:, rank:] / jnp.sqrt(pivots)


def refine_kernel(
    place_ref, mine_ref, core_ref, chan_ref, both_ref, start_ref, samples_ref, out_ref, gram_ref
):
    core, half = place_ref[0], place_ref[1]
    near = jnp.where(core == 0, mine_ref[...], core_ref[...])
    near_next = jnp.where(core == 0, core_ref[...], mine_ref[...])
    far = jnp.where(core == 0, chan_ref[...], both_ref[...])
    far_next = jnp.where(core == 0, both_ref[...], chan_ref[...])
    packed = jnp.concatenate(
        [
            jnp.where(half == 0, near, far),
            jnp.where(half == 0, far, near),
            jnp.where(half == 0, near_next, far_next),
            jnp.where(half == 0, far_next, near_next),
        ],
        axis=0,
    )
    gram_ref[...] = unpacked(packed)
    basis = start_ref[...]
    for _ in range(ITERS):
        image = jnp.dot(gram_ref[...], basis, precision=HIGHEST, preferred_element_type=jnp.float32)
        compact = lax.dot_general(
            image,
            image,
            (((0,), (0,)), ((), ())),
            precision=HIGHEST,
            preferred_element_type=jnp.float32,
        )
        basis = dot_nt(image, inverse_cholesky(compact), HIGHEST)
    basis_high, basis_low = halves(basis)
    left = jnp.concatenate([basis_high, basis_low, basis_high], axis=1)
    rank = basis.shape[1]
    for first in range(0, samples_ref.shape[1], STEP):
        columns = slice(first, first + STEP)
        samples_high, samples_low = halves(samples_ref[:, columns])
        both = lax.dot_general(
            left[:, : 2 * rank],
            samples_high,
            (((0,), (0,)), ((), ())),
            preferred_element_type=jnp.float32,
        )
        coefficients = both[:rank] + both[rank:]
        coefficients += lax.dot_general(
            basis_high,
            samples_low,
            (((0,), (0,)), ((), ())),
            preferred_element_type=jnp.float32,
        )
        high, low = halves(coefficients)
        out_ref[:, columns] = jnp.dot(
            left,
            jnp.concatenate([high, high, low], axis=0),
            preferred_element_type=jnp.float32,
        )


def denoised_band(place, quarters, start, samples):
    channels = start.shape[0]
    return pl.pallas_call(
        refine_kernel,
        in_specs=[pl.BlockSpec(memory_space=pltpu.SMEM)]
        + [pl.BlockSpec(memory_space=pltpu.VMEM)] * 6,
        out_specs=pl.BlockSpec(memory_space=pltpu.VMEM),
        out_shape=jax.ShapeDtypeStruct(samples.shape, jnp.float32),
        scratch_shapes=[pltpu.VMEM((channels, channels), jnp.float32)],
        compiler_params=pltpu.CompilerParams(vmem_limit_bytes=VMEM_LIMIT),
        name="denoised_band",
    )(place, *quarters, start, samples)


def shards(raw_strain, fir_taps, start_basis):
    own, samples = raw_strain.shape
    bands = fir_taps.shape[0]
    chan_count, tm_count = lax.axis_size("chan"), lax.axis_size("tm")
    channels = own * chan_count
    place, core = lax.axis_index("chan"), lax.axis_index("tm") % 2
    half = place % 2
    rim_piece = raw_strain[:, samples - RIM :]
    before = lax.ppermute(rim_piece, "tm", [(i, i + 1) for i in range(tm_count - 1)])
    table = filter_table(fir_taps)

    decimated = filtered(raw_strain, before, table, chan_count)
    decimated = lax.all_to_all(decimated, "chan", 0, 0, tiled=True).reshape(channels, -1)
    kept, sent = band_gram(core, decimated)

    pair = (kept + swapped(sent, "tm", 1)).reshape(2, 80, 128)
    sent = swapped(lax.dynamic_index_in_dim(pair, 1 - half, 0, False), "chan", 1)
    quarter = lax.dynamic_index_in_dim(pair, half, 0, False) + sent
    quarter = quarter + swapped(quarter, "tm", 2)
    others = [swapped(quarter, "tm", distance) for distance in (4, 8, 12)]
    quarter = (quarter + others[0]) + (others[1] + others[2])

    everyone = range(chan_count * tm_count)
    across = [(i, i ^ (tm_count + 1)) for i in everyone]
    four = (
        quarter,
        swapped(quarter, "tm", 1),
        swapped(quarter, "chan", 1),
        lax.ppermute(quarter, ("chan", "tm"), across),
    )
    start = lax.dynamic_index_in_dim(start_basis, place // 2, 0, False)
    result = denoised_band(jnp.stack([core, half]), four, start, decimated)

    result = lax.all_to_all(result.reshape(chan_count, own, -1), "chan", 0, 0, tiled=True)
    result = jnp.transpose(result.reshape(bands, chan_count // bands, own, -1), (0, 2, 1, 3))
    return result.reshape(bands, own, samples // 4)


def solution(mesh):
    placed = (P("chan", "tm"), P(), P())
    return jax.shard_map(
        shards, mesh=mesh, in_specs=placed, out_specs=P(None, "chan", "tm"), check_vma=False
    )
```

```python
import jax
import jax.numpy as jnp
from jax import lax
from jax.experimental import pallas as pl
from jax.experimental.pallas import tpu as pltpu
from jax.sharding import PartitionSpec as P

ITERS = 3
RIM = 128
STEP = 512
WINDOW = STEP + RIM
HIGHEST = lax.Precision.HIGHEST
VMEM_LIMIT = 24 * 1024 * 1024
SENT = jnp.float16
RESULT_SENT = jnp.float32
POWERS = (14,) * 9 + (8, 4, 2, 1)


def swapped(block, axis, distance):
    route = [(i, i ^ distance) for i in range(lax.axis_size(axis))]
    return lax.ppermute(block, axis, route)


def dot_nt(a, b, precision=None):
    return lax.dot_general(
        a, b, (((1,), (1,)), ((), ())), precision=precision, preferred_element_type=jnp.float32
    )


def halves(value):
    high = value.astype(jnp.bfloat16)
    return high, (value - high.astype(jnp.float32)).astype(jnp.bfloat16)


def table_kernel(taps_ref, table_ref):
    for b in range(taps_ref.shape[0]):
        row = jnp.concatenate(
            [taps_ref[b].astype(jnp.float32), jnp.zeros((1, STEP), jnp.float32)], axis=1
        )
        table = pltpu.roll(jnp.broadcast_to(row, (128, WINDOW)), 4, 1, stride=4, stride_axis=0)
        table_ref[128 * b : 128 * b + 128, :] = table.astype(table_ref.dtype)


def filter_table(fir_taps):
    return pl.pallas_call(
        table_kernel,
        out_shape=jax.ShapeDtypeStruct((128 * fir_taps.shape[0], WINDOW), fir_taps.dtype),
        compiler_params=pltpu.CompilerParams(vmem_limit_bytes=16 * 1024 * 1024),
        name="filter_table",
    )(fir_taps[:, None, :])


def powers_below(value):
    value = jnp.maximum(value, 2.0**-100)
    factors = []
    for power in POWERS:
        factor = jnp.where(
            value >= 2.0**power, 2.0**power, jnp.where(value < 2.0**-power, 2.0**-power, 1.0)
        )
        value = value / factor
        factors.append(factor)
    return factors


def product(factors):
    total = factors[0]
    for factor in factors[1:]:
        total = total * factor
    return total


def on_lanes(factors, shape):
    lanes = lax.broadcasted_iota(jnp.int32, shape, len(shape) - 1)
    result = jnp.ones(shape, jnp.float32)
    for number, factor in enumerate(factors):
        result = jnp.where(lanes == number, factor, result)
    return result


def off_lanes(row):
    return product([row[..., number : number + 1] for number in range(len(POWERS))])


def filter_kernel(raw_ref, before_ref, table_ref, out_ref, extended_ref):
    own, samples = raw_ref.shape
    receivers, _, width = out_ref.shape
    part = width - 128
    largest = jnp.max(jnp.abs(raw_ref[...].astype(jnp.float32)), keepdims=True)
    before = jnp.max(jnp.abs(before_ref[...].astype(jnp.float32)), keepdims=True)
    tap = jnp.max(jnp.abs(table_ref[...].astype(jnp.float32)), keepdims=True)
    factors = powers_below(jnp.maximum(largest, before) * tap * 2.0**-7)
    scale = 1.0 / product(factors)
    marks = on_lanes(factors, (own, 128))
    for i in range(receivers):
        out_ref[i, :, part:] = marks
    extended_ref[:, :RIM] = before_ref[...]
    extended_ref[:, RIM:] = raw_ref[...]
    blocks = samples // STEP
    windows = jnp.concatenate(
        [extended_ref[:, STEP * m : STEP * m + WINDOW] for m in range(blocks)], axis=0
    )
    bands = table_ref.shape[0] // 128
    share = part // 128
    for pair in range(bands // 2):
        both = dot_nt(windows, table_ref[256 * pair : 256 * pair + 256, :]) * scale
        for b in range(2):
            for m in range(blocks):
                place = (2 * pair + b) * (receivers // bands) + m // share
                first = 128 * (m % share)
                out_ref[place, :, first : first + 128] = both[
                    m * own : (m + 1) * own, 128 * b : 128 * b + 128
                ]


def filtered(raw_strain, before, table, receivers):
    own, samples = raw_strain.shape
    part = table.shape[0] // 128 * (samples // 4) // receivers
    return pl.pallas_call(
        filter_kernel,
        out_shape=jax.ShapeDtypeStruct((receivers, own, part + 128), jnp.float32),
        scratch_shapes=[pltpu.VMEM((own, samples + RIM), raw_strain.dtype)],
        compiler_params=pltpu.CompilerParams(vmem_limit_bytes=VMEM_LIMIT),
        name="filtered",
    )(raw_strain, before, table)


def gram_kernel(core_ref, message_ref, kept_ref, sent_ref, samples_ref, packed_ref):
    core = core_ref[0]
    count = packed_ref.shape[0] // 2
    lanes = lax.broadcasted_iota(jnp.int32, (64, 128), 1)
    sources, own, width = message_ref.shape
    for i in range(sources):
        unit = off_lanes(message_ref[i, 0:1, width - 128 :])
        samples_ref[i * own : (i + 1) * own, :] = message_ref[i, :, : width - 128] * unit
    high, low = halves(samples_ref[...])
    gram = dot_nt(high, high) + dot_nt(high, low) + dot_nt(low, high)
    packed_ref[0:64, :] = gram[0:64, 0:128]
    packed_ref[64:128, :] = gram[0:64, 128:256]
    packed_ref[128:192, :] = gram[64:128, 128:256]
    packed_ref[192:256, :] = gram[128:192, 128:256]
    last = pltpu.roll(gram[192:256, 128:256], 64, 1)
    packed_ref[256:320, :] = jnp.where(lanes < 64, last, gram[64:128, 0:128])
    kept_ref[...] = packed_ref[pl.ds(pl.multiple_of(core * count, 8), count), :]
    sent_ref[...] = packed_ref[pl.ds(pl.multiple_of((1 - core) * count, 8), count), :]


def band_gram(core, message):
    sources, own, width = message.shape
    samples = jax.ShapeDtypeStruct((sources * own, width - 128), jnp.float32)
    half = jax.ShapeDtypeStruct((160, 128), jnp.float32)
    return pl.pallas_call(
        gram_kernel,
        in_specs=[
            pl.BlockSpec(memory_space=pltpu.SMEM),
            pl.BlockSpec(memory_space=pltpu.VMEM),
        ],
        out_shape=[half, half, samples],
        scratch_shapes=[pltpu.VMEM((320, 128), jnp.float32)],
        compiler_params=pltpu.CompilerParams(vmem_limit_bytes=VMEM_LIMIT),
        name="band_gram",
    )(core.reshape(1), message)


def unpacked(packed):
    first, corner = packed[0:64], packed[256:320]
    upper = jnp.concatenate(
        [first, jnp.concatenate([first.T[64:128], corner[:, 64:128]], axis=1)], axis=0
    )
    third = packed[192:256]
    lower = jnp.concatenate(
        [third, jnp.concatenate([third.T[64:128], corner[:, 0:64]], axis=1)], axis=0
    )
    across = packed[64:192]
    return jnp.concatenate(
        [
            jnp.concatenate([upper, across], axis=1),
            jnp.concatenate([across.T, lower], axis=1),
        ],
        axis=0,
    )


def decimated_gram(core, windows, table):
    channels, samples = windows.shape
    bands = table.shape[0] // 128
    half = jax.ShapeDtypeStruct((bands, 160, 128), jnp.float32)
    half_spec = pl.BlockSpec((2, 160, 128), lambda b: (b, 0, 0))
    count = (samples - RIM) // 4
    piece = jax.ShapeDtypeStruct((bands, channels, count), jnp.bfloat16)
    piece_spec = pl.BlockSpec((2, channels, count), lambda b: (b, 0, 0))
    return pl.pallas_call(
        gram_kernel,
        grid=(bands // 2,),
        in_specs=[
            pl.BlockSpec(memory_space=pltpu.SMEM),
            pl.BlockSpec((channels, samples), lambda b: (0, 0)),
            pl.BlockSpec((256, WINDOW), lambda b: (b, 0)),
        ],
        out_specs=[half_spec, half_spec, piece_spec, piece_spec],
        out_shape=[half, half, piece, piece],
        scratch_shapes=[pltpu.VMEM((320, 128), jnp.float32)],
        compiler_params=pltpu.CompilerParams(vmem_limit_bytes=VMEM_LIMIT),
        name="decimated_gram",
    )(core.reshape(1), windows, table)


def inverse_cholesky(compact):
    rank = compact.shape[0]
    rows = lax.broadcasted_iota(jnp.int32, (rank, rank), 0)
    columns = lax.broadcasted_iota(jnp.int32, (rank, rank), 1)
    unit = (rows == columns).astype(jnp.float32)
    both = jnp.concatenate([compact, unit], axis=1)
    below = lax.broadcasted_iota(jnp.int32, both.shape, 0)
    for block in range(0, rank, 8):
        spread = [
            jnp.broadcast_to(both[:, block + p : block + p + 1], both.shape) for p in range(8)
        ]
        for p in range(8):
            j = block + p
            column = spread[p]
            factor = jnp.where(below > j, column * (1.0 / column[j : j + 1, :]), 0.0)
            both = both - factor * both[j : j + 1, :]
            for q in range(p + 1, 8):
                spread[q] = spread[q] - factor * spread[q][j : j + 1, :]
    pivots = jnp.sum(unit * both[:, :rank], axis=1, keepdims=True)
    return both[:, rank:] / jnp.sqrt(pivots)


def refine_kernel(
    place_ref, mine_ref, core_ref, chan_ref, both_ref, start_ref, samples_ref, out_ref, gram_ref
):
    core, half = place_ref[0], place_ref[1]
    near = jnp.where(core == 0, mine_ref[...], core_ref[...])
    near_next = jnp.where(core == 0, core_ref[...], mine_ref[...])
    far = jnp.where(core == 0, chan_ref[...], both_ref[...])
    far_next = jnp.where(core == 0, both_ref[...], chan_ref[...])
    packed = jnp.concatenate(
        [
            jnp.where(half == 0, near, far),
            jnp.where(half == 0, far, near),
            jnp.where(half == 0, near_next, far_next),
            jnp.where(half == 0, far_next, near_next),
        ],
        axis=0,
    )
    gram_ref[...] = unpacked(packed)
    basis = start_ref[...]
    for _ in range(ITERS):
        image = jnp.dot(gram_ref[...], basis, precision=HIGHEST, preferred_element_type=jnp.float32)
        compact = lax.dot_general(
            image,
            image,
            (((0,), (0,)), ((), ())),
            precision=HIGHEST,
            preferred_element_type=jnp.float32,
        )
        basis = dot_nt(image, inverse_cholesky(compact), HIGHEST)
    rows = lax.broadcasted_iota(jnp.int32, gram_ref.shape, 0)
    columns = lax.broadcasted_iota(jnp.int32, gram_ref.shape, 1)
    trace = jnp.sum(jnp.where(rows == columns, gram_ref[...], 0.0), keepdims=True)
    factors = powers_below(jnp.sqrt(trace) * 2.0**-14)
    scale = 1.0 / product(factors)
    part = samples_ref.shape[1]
    out_ref[:, part:] = on_lanes(factors, (out_ref.shape[0], 128))
    basis_high, basis_low = halves(basis)
    left = jnp.concatenate([basis_high, basis_low, basis_high], axis=1)
    rank = basis.shape[1]
    for first in range(0, part, STEP):
        columns = slice(first, first + STEP)
        samples_high, samples_low = halves(samples_ref[:, columns])
        both = lax.dot_general(
            left[:, : 2 * rank],
            samples_high,
            (((0,), (0,)), ((), ())),
            preferred_element_type=jnp.float32,
        )
        coefficients = both[:rank] + both[rank:]
        coefficients += lax.dot_general(
            basis_high,
            samples_low,
            (((0,), (0,)), ((), ())),
            preferred_element_type=jnp.float32,
        )
        high, low = halves(coefficients * scale)
        out_ref[:, columns] = jnp.dot(
            left,
            jnp.concatenate([high, high, low], axis=0),
            preferred_element_type=jnp.float32,
        )


def denoised_band(place, quarters, start, samples):
    channels = start.shape[0]
    return pl.pallas_call(
        refine_kernel,
        in_specs=[pl.BlockSpec(memory_space=pltpu.SMEM)]
        + [pl.BlockSpec(memory_space=pltpu.VMEM)] * 6,
        out_specs=pl.BlockSpec(memory_space=pltpu.VMEM),
        out_shape=jax.ShapeDtypeStruct((channels, samples.shape[1] + 128), jnp.float32),
        scratch_shapes=[pltpu.VMEM((channels, channels), jnp.float32)],
        compiler_params=pltpu.CompilerParams(vmem_limit_bytes=VMEM_LIMIT),
        name="denoised_band",
    )(place, *quarters, start, samples)


def restore_kernel(message_ref, out_ref):
    shares, _, width = message_ref.shape
    part = width - 128
    for i in range(shares):
        unit = off_lanes(message_ref[i, 0:1, part:])
        out_ref[0, :, i * part : (i + 1) * part] = message_ref[i, :, :part] * unit


def restored(message, bands):
    sources, own, width = message.shape
    shares = sources // bands
    total = shares * (width - 128)
    return pl.pallas_call(
        restore_kernel,
        grid=(bands,),
        in_specs=[pl.BlockSpec((shares, own, width), lambda b: (b, 0, 0))],
        out_specs=pl.BlockSpec((1, own, total), lambda b: (b, 0, 0)),
        out_shape=jax.ShapeDtypeStruct((bands, own, total), jnp.float32),
        compiler_params=pltpu.CompilerParams(vmem_limit_bytes=VMEM_LIMIT),
        name="restored",
    )(message)


def shards(raw_strain, fir_taps, start_basis):
    own, samples = raw_strain.shape
    bands = fir_taps.shape[0]
    chan_count, tm_count = lax.axis_size("chan"), lax.axis_size("tm")
    place, core = lax.axis_index("chan"), lax.axis_index("tm") % 2
    half = place % 2
    rim_piece = raw_strain[:, samples - RIM :]
    before = lax.ppermute(rim_piece, "tm", [(i, i + 1) for i in range(tm_count - 1)])
    table = filter_table(fir_taps)

    message = filtered(raw_strain, before, table, chan_count).astype(SENT)
    message = lax.all_to_all(message, "chan", 0, 0, tiled=True).astype(jnp.float32)
    kept, sent, decimated = band_gram(core, message)

    pair = (kept + swapped(sent, "tm", 1)).reshape(2, 80, 128)
    sent = swapped(lax.dynamic_index_in_dim(pair, 1 - half, 0, False), "chan", 1)
    quarter = lax.dynamic_index_in_dim(pair, half, 0, False) + sent
    quarter = quarter + swapped(quarter, "tm", 2)
    others = [swapped(quarter, "tm", distance) for distance in (4, 8, 12)]
    quarter = (quarter + others[0]) + (others[1] + others[2])

    everyone = range(chan_count * tm_count)
    across = [(i, i ^ (tm_count + 1)) for i in everyone]
    four = (
        quarter,
        swapped(quarter, "tm", 1),
        swapped(quarter, "chan", 1),
        lax.ppermute(quarter, ("chan", "tm"), across),
    )
    start = lax.dynamic_index_in_dim(start_basis, place // 2, 0, False)
    result = denoised_band(jnp.stack([core, half]), four, start, decimated)

    result = result.reshape(chan_count, own, -1).astype(RESULT_SENT)
    result = lax.all_to_all(result, "chan", 0, 0, tiled=True)
    return restored(result.astype(jnp.float32), bands)


def solution(mesh):
    placed = (P("chan", "tm"), P(), P())
    return jax.shard_map(
        shards, mesh=mesh, in_specs=placed, out_specs=P(None, "chan", "tm"), check_vma=False
    )
```

```python
import jax
import jax.numpy as jnp
from jax import lax
from jax.experimental import pallas as pl
from jax.experimental.pallas import tpu as pltpu
from jax.sharding import PartitionSpec as P

ITERS = 3
RIM = 128
STEP = 512
WINDOW = STEP + RIM
HIGHEST = lax.Precision.HIGHEST
VMEM_LIMIT = 24 * 1024 * 1024
SENT = jnp.float16
POWERS = (14,) * 9 + (8, 4, 2, 1)


def swapped(block, axis, distance):
    route = [(i, i ^ distance) for i in range(lax.axis_size(axis))]
    return lax.ppermute(block, axis, route)


def dot_nt(a, b, precision=None):
    return lax.dot_general(
        a, b, (((1,), (1,)), ((), ())), precision=precision, preferred_element_type=jnp.float32
    )


def halves(value):
    high = value.astype(jnp.bfloat16)
    return high, (value - high.astype(jnp.float32)).astype(jnp.bfloat16)


def table_kernel(taps_ref, table_ref):
    for b in range(taps_ref.shape[0]):
        row = jnp.concatenate(
            [taps_ref[b].astype(jnp.float32), jnp.zeros((1, STEP), jnp.float32)], axis=1
        )
        table = pltpu.roll(jnp.broadcast_to(row, (128, WINDOW)), 4, 1, stride=4, stride_axis=0)
        table_ref[128 * b : 128 * b + 128, :] = table.astype(table_ref.dtype)


def filter_table(fir_taps):
    return pl.pallas_call(
        table_kernel,
        out_shape=jax.ShapeDtypeStruct((128 * fir_taps.shape[0], WINDOW), fir_taps.dtype),
        compiler_params=pltpu.CompilerParams(vmem_limit_bytes=16 * 1024 * 1024),
        name="filter_table",
    )(fir_taps[:, None, :])


def powers_below(value):
    value = jnp.maximum(value, 2.0**-100)
    factors = []
    for power in POWERS:
        factor = jnp.where(
            value >= 2.0**power, 2.0**power, jnp.where(value < 2.0**-power, 2.0**-power, 1.0)
        )
        value = value / factor
        factors.append(factor)
    return factors


def product(factors):
    total = factors[0]
    for factor in factors[1:]:
        total = total * factor
    return total


def on_lanes(factors, shape):
    lanes = lax.broadcasted_iota(jnp.int32, shape, len(shape) - 1)
    result = jnp.ones(shape, jnp.float32)
    for number, factor in enumerate(factors):
        result = jnp.where(lanes == number, factor, result)
    return result


def off_lanes(row):
    return product([row[..., number : number + 1] for number in range(len(POWERS))])


def squared(value):
    return value * jnp.abs(value)


def unsquared(value):
    root = jnp.sqrt(jnp.abs(value))
    return jnp.where(value < 0, -root, root)


def filter_kernel(raw_ref, before_ref, table_ref, out_ref, extended_ref):
    own, samples = raw_ref.shape
    receivers, _, width = out_ref.shape
    part = width - 128
    extended_ref[:, :RIM] = before_ref[...]
    extended_ref[:, RIM:] = raw_ref[...]
    blocks = samples // STEP
    windows = jnp.concatenate(
        [extended_ref[:, STEP * m : STEP * m + WINDOW] for m in range(blocks)], axis=0
    )
    bands = table_ref.shape[0] // 128
    share = part // 128
    peaks = []
    for pair in range(bands // 2):
        both = dot_nt(windows, table_ref[256 * pair : 256 * pair + 256, :])
        for b in range(2):
            largest = jnp.max(jnp.abs(both[:, 128 * b : 128 * b + 128]), axis=0, keepdims=True)
            peaks.append(jnp.max(largest, axis=1, keepdims=True))
            for m in range(blocks):
                place = (2 * pair + b) * (receivers // bands) + m // share
                first = 128 * (m % share)
                out_ref[place, :, first : first + 128] = both[
                    m * own : (m + 1) * own, 128 * b : 128 * b + 128
                ]
    factors = powers_below(jnp.concatenate(peaks, axis=0) * 2.0**-6)
    scale = 1.0 / product(factors)
    for i in range(receivers):
        b = i // (receivers // bands)
        out_ref[i, :, :part] = squared(out_ref[i, :, :part] * scale[b : b + 1, :])
        out_ref[i, :, part:] = on_lanes([factor[b : b + 1, :] for factor in factors], (own, 128))


def filtered(raw_strain, before, table, receivers):
    own, samples = raw_strain.shape
    part = table.shape[0] // 128 * (samples // 4) // receivers
    return pl.pallas_call(
        filter_kernel,
        out_shape=jax.ShapeDtypeStruct((receivers, own, part + 128), jnp.float32),
        scratch_shapes=[pltpu.VMEM((own, samples + RIM), raw_strain.dtype)],
        compiler_params=pltpu.CompilerParams(vmem_limit_bytes=VMEM_LIMIT),
        name="filtered",
    )(raw_strain, before, table)


def gram_kernel(core_ref, message_ref, kept_ref, sent_ref, samples_ref, packed_ref):
    core = core_ref[0]
    count = packed_ref.shape[0] // 2
    lanes = lax.broadcasted_iota(jnp.int32, (64, 128), 1)
    sources, own, width = message_ref.shape
    for i in range(sources):
        unit = off_lanes(message_ref[i, 0:1, width - 128 :])
        samples_ref[i * own : (i + 1) * own, :] = (
            unsquared(message_ref[i, :, : width - 128]) * unit
        )
    high, low = halves(samples_ref[...])
    gram = dot_nt(high, high) + dot_nt(high, low) + dot_nt(low, high)
    packed_ref[0:64, :] = gram[0:64, 0:128]
    packed_ref[64:128, :] = gram[0:64, 128:256]
    packed_ref[128:192, :] = gram[64:128, 128:256]
    packed_ref[192:256, :] = gram[128:192, 128:256]
    last = pltpu.roll(gram[192:256, 128:256], 64, 1)
    packed_ref[256:320, :] = jnp.where(lanes < 64, last, gram[64:128, 0:128])
    kept_ref[...] = packed_ref[pl.ds(pl.multiple_of(core * count, 8), count), :]
    sent_ref[...] = packed_ref[pl.ds(pl.multiple_of((1 - core) * count, 8), count), :]


def band_gram(core, message):
    sources, own, width = message.shape
    samples = jax.ShapeDtypeStruct((sources * own, width - 128), jnp.float32)
    half = jax.ShapeDtypeStruct((160, 128), jnp.float32)
    return pl.pallas_call(
        gram_kernel,
        in_specs=[
            pl.BlockSpec(memory_space=pltpu.SMEM),
            pl.BlockSpec(memory_space=pltpu.VMEM),
        ],
        out_shape=[half, half, samples],
        scratch_shapes=[pltpu.VMEM((320, 128), jnp.float32)],
        compiler_params=pltpu.CompilerParams(vmem_limit_bytes=VMEM_LIMIT),
        name="band_gram",
    )(core.reshape(1), message)


def unpacked(packed):
    first, corner = packed[0:64], packed[256:320]
    upper = jnp.concatenate(
        [first, jnp.concatenate([first.T[64:128], corner[:, 64:128]], axis=1)], axis=0
    )
    third = packed[192:256]
    lower = jnp.concatenate(
        [third, jnp.concatenate([third.T[64:128], corner[:, 0:64]], axis=1)], axis=0
    )
    across = packed[64:192]
    return jnp.concatenate(
        [
            jnp.concatenate([upper, across], axis=1),
            jnp.concatenate([across.T, lower], axis=1),
        ],
        axis=0,
    )


def decimated_gram(core, windows, table):
    channels, samples = windows.shape
    bands = table.shape[0] // 128
    half = jax.ShapeDtypeStruct((bands, 160, 128), jnp.float32)
    half_spec = pl.BlockSpec((2, 160, 128), lambda b: (b, 0, 0))
    count = (samples - RIM) // 4
    piece = jax.ShapeDtypeStruct((bands, channels, count), jnp.bfloat16)
    piece_spec = pl.BlockSpec((2, channels, count), lambda b: (b, 0, 0))
    return pl.pallas_call(
        gram_kernel,
        grid=(bands // 2,),
        in_specs=[
            pl.BlockSpec(memory_space=pltpu.SMEM),
            pl.BlockSpec((channels, samples), lambda b: (0, 0)),
            pl.BlockSpec((256, WINDOW), lambda b: (b, 0)),
        ],
        out_specs=[half_spec, half_spec, piece_spec, piece_spec],
        out_shape=[half, half, piece, piece],
        scratch_shapes=[pltpu.VMEM((320, 128), jnp.float32)],
        compiler_params=pltpu.CompilerParams(vmem_limit_bytes=VMEM_LIMIT),
        name="decimated_gram",
    )(core.reshape(1), windows, table)


def inverse_cholesky(compact):
    rank = compact.shape[0]
    rows = lax.broadcasted_iota(jnp.int32, (rank, rank), 0)
    columns = lax.broadcasted_iota(jnp.int32, (rank, rank), 1)
    unit = (rows == columns).astype(jnp.float32)
    both = jnp.concatenate([compact, unit], axis=1)
    below = lax.broadcasted_iota(jnp.int32, both.shape, 0)
    for block in range(0, rank, 8):
        spread = [
            jnp.broadcast_to(both[:, block + p : block + p + 1], both.shape) for p in range(8)
        ]
        for p in range(8):
            j = block + p
            column = spread[p]
            factor = jnp.where(below > j, column * (1.0 / column[j : j + 1, :]), 0.0)
            both = both - factor * both[j : j + 1, :]
            for q in range(p + 1, 8):
                spread[q] = spread[q] - factor * spread[q][j : j + 1, :]
    pivots = jnp.sum(unit * both[:, :rank], axis=1, keepdims=True)
    return both[:, rank:] / jnp.sqrt(pivots)


def refine_kernel(
    place_ref, mine_ref, core_ref, chan_ref, both_ref, start_ref, samples_ref, out_ref, gram_ref
):
    core, half = place_ref[0], place_ref[1]
    near = jnp.where(core == 0, mine_ref[...], core_ref[...])
    near_next = jnp.where(core == 0, core_ref[...], mine_ref[...])
    far = jnp.where(core == 0, chan_ref[...], both_ref[...])
    far_next = jnp.where(core == 0, both_ref[...], chan_ref[...])
    packed = jnp.concatenate(
        [
            jnp.where(half == 0, near, far),
            jnp.where(half == 0, far, near),
            jnp.where(half == 0, near_next, far_next),
            jnp.where(half == 0, far_next, near_next),
        ],
        axis=0,
    )
    gram_ref[...] = unpacked(packed)
    basis = start_ref[...]
    for _ in range(ITERS):
        image = jnp.dot(gram_ref[...], basis, precision=HIGHEST, preferred_element_type=jnp.float32)
        compact = lax.dot_general(
            image,
            image,
            (((0,), (0,)), ((), ())),
            precision=HIGHEST,
            preferred_element_type=jnp.float32,
        )
        basis = dot_nt(image, inverse_cholesky(compact), HIGHEST)
    part = samples_ref.shape[1]
    peak = jnp.zeros((1, STEP), jnp.float32)
    basis_high, basis_low = halves(basis)
    left = jnp.concatenate([basis_high, basis_low, basis_high], axis=1)
    rank = basis.shape[1]
    for first in range(0, part, STEP):
        columns = slice(first, first + STEP)
        samples_high, samples_low = halves(samples_ref[:, columns])
        both = lax.dot_general(
            left[:, : 2 * rank],
            samples_high,
            (((0,), (0,)), ((), ())),
            preferred_element_type=jnp.float32,
        )
        coefficients = both[:rank] + both[rank:]
        coefficients += lax.dot_general(
            basis_high,
            samples_low,
            (((0,), (0,)), ((), ())),
            preferred_element_type=jnp.float32,
        )
        high, low = halves(coefficients)
        result = jnp.dot(
            left,
            jnp.concatenate([high, high, low], axis=0),
            preferred_element_type=jnp.float32,
        )
        out_ref[:, columns] = result
        peak = jnp.maximum(peak, jnp.max(jnp.abs(result), axis=0, keepdims=True))
    factors = powers_below(jnp.max(peak, axis=1, keepdims=True) * 2.0**-6)
    scale = 1.0 / product(factors)
    for first in range(0, part, STEP):
        columns = slice(first, first + STEP)
        out_ref[:, columns] = squared(out_ref[:, columns] * scale)
    out_ref[:, part:] = on_lanes(factors, (out_ref.shape[0], 128))


def denoised_band(place, quarters, start, samples):
    channels = start.shape[0]
    return pl.pallas_call(
        refine_kernel,
        in_specs=[pl.BlockSpec(memory_space=pltpu.SMEM)]
        + [pl.BlockSpec(memory_space=pltpu.VMEM)] * 6,
        out_specs=pl.BlockSpec(memory_space=pltpu.VMEM),
        out_shape=jax.ShapeDtypeStruct((channels, samples.shape[1] + 128), jnp.float32),
        scratch_shapes=[pltpu.VMEM((channels, channels), jnp.float32)],
        compiler_params=pltpu.CompilerParams(vmem_limit_bytes=VMEM_LIMIT),
        name="denoised_band",
    )(place, *quarters, start, samples)


def restore_kernel(message_ref, out_ref):
    shares, _, width = message_ref.shape
    part = width - 128
    for i in range(shares):
        unit = off_lanes(message_ref[i, 0:1, part:])
        out_ref[0, :, i * part : (i + 1) * part] = (
            unsquared(message_ref[i, :, :part]) * unit
        )


def restored(message, bands):
    sources, own, width = message.shape
    shares = sources // bands
    total = shares * (width - 128)
    return pl.pallas_call(
        restore_kernel,
        grid=(bands,),
        in_specs=[pl.BlockSpec((shares, own, width), lambda b: (b, 0, 0))],
        out_specs=pl.BlockSpec((1, own, total), lambda b: (b, 0, 0)),
        out_shape=jax.ShapeDtypeStruct((bands, own, total), jnp.float32),
        compiler_params=pltpu.CompilerParams(vmem_limit_bytes=VMEM_LIMIT),
        name="restored",
    )(message)


def shards(raw_strain, fir_taps, start_basis):
    own, samples = raw_strain.shape
    bands = fir_taps.shape[0]
    chan_count, tm_count = lax.axis_size("chan"), lax.axis_size("tm")
    place, core = lax.axis_index("chan"), lax.axis_index("tm") % 2
    half = place % 2
    rim_piece = raw_strain[:, samples - RIM :]
    before = lax.ppermute(rim_piece, "tm", [(i, i + 1) for i in range(tm_count - 1)])
    table = filter_table(fir_taps)

    message = filtered(raw_strain, before, table, chan_count).astype(SENT)
    message = lax.all_to_all(message, "chan", 0, 0, tiled=True).astype(jnp.float32)
    kept, sent, decimated = band_gram(core, message)

    pair = (kept + swapped(sent, "tm", 1)).reshape(2, 80, 128)
    sent = swapped(lax.dynamic_index_in_dim(pair, 1 - half, 0, False), "chan", 1)
    quarter = lax.dynamic_index_in_dim(pair, half, 0, False) + sent
    quarter = quarter + swapped(quarter, "tm", 2)
    others = [swapped(quarter, "tm", distance) for distance in (4, 8, 12)]
    quarter = (quarter + others[0]) + (others[1] + others[2])

    everyone = range(chan_count * tm_count)
    across = [(i, i ^ (tm_count + 1)) for i in everyone]
    four = (
        quarter,
        swapped(quarter, "tm", 1),
        swapped(quarter, "chan", 1),
        lax.ppermute(quarter, ("chan", "tm"), across),
    )
    start = lax.dynamic_index_in_dim(start_basis, place // 2, 0, False)
    result = denoised_band(jnp.stack([core, half]), four, start, decimated)

    result = result.reshape(chan_count, own, -1).astype(SENT)
    result = lax.all_to_all(result, "chan", 0, 0, tiled=True)
    return restored(result.astype(jnp.float32), bands)


def solution(mesh):
    placed = (P("chan", "tm"), P(), P())
    return jax.shard_map(
        shards, mesh=mesh, in_specs=placed, out_specs=P(None, "chan", "tm"), check_vma=False
    )
```

```python
import jax
import jax.numpy as jnp
from jax import lax
from jax.experimental import pallas as pl
from jax.experimental.pallas import tpu as pltpu
from jax.sharding import PartitionSpec as P

ITERS = 3
RIM = 128
STEP = 512
WINDOW = STEP + RIM
HIGHEST = lax.Precision.HIGHEST
VMEM_LIMIT = 24 * 1024 * 1024
SENT = jnp.float16
POWERS = (14,) * 9 + (8, 4, 2, 1)


def swapped(block, axis, distance):
    route = [(i, i ^ distance) for i in range(lax.axis_size(axis))]
    return lax.ppermute(block, axis, route)


def dot_nt(a, b, precision=None):
    return lax.dot_general(
        a, b, (((1,), (1,)), ((), ())), precision=precision, preferred_element_type=jnp.float32
    )


def halves(value):
    high = value.astype(jnp.bfloat16)
    return high, (value - high.astype(jnp.float32)).astype(jnp.bfloat16)


def table_kernel(taps_ref, table_ref):
    for b in range(taps_ref.shape[0]):
        row = jnp.concatenate(
            [taps_ref[b].astype(jnp.float32), jnp.zeros((1, STEP), jnp.float32)], axis=1
        )
        table = pltpu.roll(jnp.broadcast_to(row, (128, WINDOW)), 4, 1, stride=4, stride_axis=0)
        table_ref[128 * b : 128 * b + 128, :] = table.astype(table_ref.dtype)


def filter_table(fir_taps):
    return pl.pallas_call(
        table_kernel,
        out_shape=jax.ShapeDtypeStruct((128 * fir_taps.shape[0], WINDOW), fir_taps.dtype),
        compiler_params=pltpu.CompilerParams(vmem_limit_bytes=16 * 1024 * 1024),
        name="filter_table",
    )(fir_taps[:, None, :])


def powers_below(value):
    value = jnp.maximum(value, 2.0**-100)
    factors = []
    for power in POWERS:
        factor = jnp.where(
            value >= 2.0**power, 2.0**power, jnp.where(value < 2.0**-power, 2.0**-power, 1.0)
        )
        value = value / factor
        factors.append(factor)
    return factors


def product(factors):
    total = factors[0]
    for factor in factors[1:]:
        total = total * factor
    return total


def on_lanes(factors, shape):
    lanes = lax.broadcasted_iota(jnp.int32, shape, len(shape) - 1)
    result = jnp.ones(shape, jnp.float32)
    for number, factor in enumerate(factors):
        result = jnp.where(lanes == number, factor, result)
    return result


def off_lanes(row):
    return product([row[..., number : number + 1] for number in range(len(POWERS))])


def squared(value):
    return value * jnp.abs(value)


def unsquared(value):
    root = jnp.sqrt(jnp.abs(value))
    return jnp.where(value < 0, -root, root)


def filter_kernel(raw_ref, before_ref, table_ref, out_ref, extended_ref):
    own, samples = raw_ref.shape
    receivers, _, width = out_ref.shape
    part = width - 128
    extended_ref[:, :RIM] = before_ref[...]
    extended_ref[:, RIM:] = raw_ref[...]
    blocks = samples // STEP
    windows = jnp.concatenate(
        [extended_ref[:, STEP * m : STEP * m + WINDOW] for m in range(blocks)], axis=0
    )
    bands = table_ref.shape[0] // 128
    share = part // 128
    peaks = []
    for pair in range(bands // 2):
        both = dot_nt(windows, table_ref[256 * pair : 256 * pair + 256, :])
        for b in range(2):
            largest = jnp.max(jnp.abs(both[:, 128 * b : 128 * b + 128]), axis=0, keepdims=True)
            peaks.append(jnp.max(largest, axis=1, keepdims=True))
            for m in range(blocks):
                place = (2 * pair + b) * (receivers // bands) + m // share
                first = 128 * (m % share)
                out_ref[place, :, first : first + 128] = both[
                    m * own : (m + 1) * own, 128 * b : 128 * b + 128
                ]
    factors = powers_below(jnp.concatenate(peaks, axis=0) * 2.0**-6)
    scale = 1.0 / product(factors)
    for i in range(receivers):
        b = i // (receivers // bands)
        out_ref[i, :, :part] = squared(out_ref[i, :, :part] * scale[b : b + 1, :])
        out_ref[i, :, part:] = on_lanes([factor[b : b + 1, :] for factor in factors], (own, 128))


def filtered(raw_strain, before, table, receivers):
    own, samples = raw_strain.shape
    part = table.shape[0] // 128 * (samples // 4) // receivers
    return pl.pallas_call(
        filter_kernel,
        out_shape=jax.ShapeDtypeStruct((receivers, own, part + 128), jnp.float32),
        scratch_shapes=[pltpu.VMEM((own, samples + RIM), raw_strain.dtype)],
        compiler_params=pltpu.CompilerParams(vmem_limit_bytes=VMEM_LIMIT),
        name="filtered",
    )(raw_strain, before, table)


def gram_kernel(core_ref, message_ref, kept_ref, sent_ref, samples_ref, packed_ref):
    core = core_ref[0]
    count = packed_ref.shape[0] // 2
    lanes = lax.broadcasted_iota(jnp.int32, (64, 128), 1)
    sources, own, width = message_ref.shape
    for i in range(sources):
        unit = off_lanes(message_ref[i, 0:1, width - 128 :])
        samples_ref[i * own : (i + 1) * own, :] = (
            unsquared(message_ref[i, :, : width - 128]) * unit
        )
    high, low = halves(samples_ref[...])
    gram = dot_nt(high, high) + dot_nt(high, low) + dot_nt(low, high)
    packed_ref[0:64, :] = gram[0:64, 0:128]
    packed_ref[64:128, :] = gram[0:64, 128:256]
    packed_ref[128:192, :] = gram[64:128, 128:256]
    packed_ref[192:256, :] = gram[128:192, 128:256]
    last = pltpu.roll(gram[192:256, 128:256], 64, 1)
    packed_ref[256:320, :] = jnp.where(lanes < 64, last, gram[64:128, 0:128])
    kept_ref[...] = packed_ref[pl.ds(pl.multiple_of(core * count, 8), count), :]
    sent_ref[...] = packed_ref[pl.ds(pl.multiple_of((1 - core) * count, 8), count), :]


def band_gram(core, message):
    sources, own, width = message.shape
    samples = jax.ShapeDtypeStruct((sources * own, width - 128), jnp.float32)
    half = jax.ShapeDtypeStruct((160, 128), jnp.float32)
    return pl.pallas_call(
        gram_kernel,
        in_specs=[
            pl.BlockSpec(memory_space=pltpu.SMEM),
            pl.BlockSpec(memory_space=pltpu.VMEM),
        ],
        out_shape=[half, half, samples],
        scratch_shapes=[pltpu.VMEM((320, 128), jnp.float32)],
        compiler_params=pltpu.CompilerParams(vmem_limit_bytes=VMEM_LIMIT),
        name="band_gram",
    )(core.reshape(1), message)


def unpacked(packed):
    first, corner = packed[0:64], packed[256:320]
    upper = jnp.concatenate(
        [first, jnp.concatenate([first.T[64:128], corner[:, 64:128]], axis=1)], axis=0
    )
    third = packed[192:256]
    lower = jnp.concatenate(
        [third, jnp.concatenate([third.T[64:128], corner[:, 0:64]], axis=1)], axis=0
    )
    across = packed[64:192]
    return jnp.concatenate(
        [
            jnp.concatenate([upper, across], axis=1),
            jnp.concatenate([across.T, lower], axis=1),
        ],
        axis=0,
    )


def decimated_gram(core, windows, table):
    channels, samples = windows.shape
    bands = table.shape[0] // 128
    half = jax.ShapeDtypeStruct((bands, 160, 128), jnp.float32)
    half_spec = pl.BlockSpec((2, 160, 128), lambda b: (b, 0, 0))
    count = (samples - RIM) // 4
    piece = jax.ShapeDtypeStruct((bands, channels, count), jnp.bfloat16)
    piece_spec = pl.BlockSpec((2, channels, count), lambda b: (b, 0, 0))
    return pl.pallas_call(
        gram_kernel,
        grid=(bands // 2,),
        in_specs=[
            pl.BlockSpec(memory_space=pltpu.SMEM),
            pl.BlockSpec((channels, samples), lambda b: (0, 0)),
            pl.BlockSpec((256, WINDOW), lambda b: (b, 0)),
        ],
        out_specs=[half_spec, half_spec, piece_spec, piece_spec],
        out_shape=[half, half, piece, piece],
        scratch_shapes=[pltpu.VMEM((320, 128), jnp.float32)],
        compiler_params=pltpu.CompilerParams(vmem_limit_bytes=VMEM_LIMIT),
        name="decimated_gram",
    )(core.reshape(1), windows, table)


def inverse_cholesky(compact):
    rank = compact.shape[0]
    rows = lax.broadcasted_iota(jnp.int32, (rank, rank), 0)
    columns = lax.broadcasted_iota(jnp.int32, (rank, rank), 1)
    unit = (rows == columns).astype(jnp.float32)
    both = jnp.concatenate([compact, unit], axis=1)
    below = lax.broadcasted_iota(jnp.int32, both.shape, 0)
    for block in range(0, rank, 8):
        spread = [
            jnp.broadcast_to(both[:, block + p : block + p + 1], both.shape) for p in range(8)
        ]
        for p in range(8):
            j = block + p
            column = spread[p]
            factor = jnp.where(below > j, column * (1.0 / column[j : j + 1, :]), 0.0)
            both = both - factor * both[j : j + 1, :]
            for q in range(p + 1, 8):
                spread[q] = spread[q] - factor * spread[q][j : j + 1, :]
    pivots = jnp.sum(unit * both[:, :rank], axis=1, keepdims=True)
    return both[:, rank:] / jnp.sqrt(pivots)


def refine_kernel(
    place_ref, mine_ref, core_ref, chan_ref, both_ref, start_ref, samples_ref, out_ref, gram_ref
):
    core, half = place_ref[0], place_ref[1]
    near = jnp.where(core == 0, mine_ref[...], core_ref[...])
    near_next = jnp.where(core == 0, core_ref[...], mine_ref[...])
    far = jnp.where(core == 0, chan_ref[...], both_ref[...])
    far_next = jnp.where(core == 0, both_ref[...], chan_ref[...])
    packed = jnp.concatenate(
        [
            jnp.where(half == 0, near, far),
            jnp.where(half == 0, far, near),
            jnp.where(half == 0, near_next, far_next),
            jnp.where(half == 0, far_next, near_next),
        ],
        axis=0,
    )
    gram_ref[...] = unpacked(packed)
    basis = start_ref[...]
    for _ in range(ITERS):
        image = jnp.dot(gram_ref[...], basis, precision=HIGHEST, preferred_element_type=jnp.float32)
        compact = lax.dot_general(
            image,
            image,
            (((0,), (0,)), ((), ())),
            precision=HIGHEST,
            preferred_element_type=jnp.float32,
        )
        basis = dot_nt(image, inverse_cholesky(compact), HIGHEST)
    part = samples_ref.shape[1]
    peak = jnp.zeros((1, STEP), jnp.float32)
    basis_high, basis_low = halves(basis)
    left = jnp.concatenate([basis_high, basis_low, basis_high], axis=1)
    rank = basis.shape[1]
    for first in range(0, part, STEP):
        columns = slice(first, first + STEP)
        samples_high, samples_low = halves(samples_ref[:, columns])
        both = lax.dot_general(
            left[:, : 2 * rank],
            samples_high,
            (((0,), (0,)), ((), ())),
            preferred_element_type=jnp.float32,
        )
        coefficients = both[:rank] + both[rank:]
        coefficients += lax.dot_general(
            basis_high,
            samples_low,
            (((0,), (0,)), ((), ())),
            preferred_element_type=jnp.float32,
        )
        high, low = halves(coefficients)
        result = jnp.dot(
            left,
            jnp.concatenate([high, high, low], axis=0),
            preferred_element_type=jnp.float32,
        )
        out_ref[:, columns] = result
        peak = jnp.maximum(peak, jnp.max(jnp.abs(result), axis=0, keepdims=True))
    factors = powers_below(jnp.max(peak, axis=1, keepdims=True) * 2.0**-6)
    scale = 1.0 / product(factors)
    for first in range(0, part, STEP):
        columns = slice(first, first + STEP)
        out_ref[:, columns] = squared(out_ref[:, columns] * scale)
    out_ref[:, part:] = on_lanes(factors, (out_ref.shape[0], 128))


def denoised_band(place, quarters, start, samples):
    channels = start.shape[0]
    return pl.pallas_call(
        refine_kernel,
        in_specs=[pl.BlockSpec(memory_space=pltpu.SMEM)]
        + [pl.BlockSpec(memory_space=pltpu.VMEM)] * 6,
        out_specs=pl.BlockSpec(memory_space=pltpu.VMEM),
        out_shape=jax.ShapeDtypeStruct((channels, samples.shape[1] + 128), jnp.float32),
        scratch_shapes=[pltpu.VMEM((channels, channels), jnp.float32)],
        compiler_params=pltpu.CompilerParams(vmem_limit_bytes=VMEM_LIMIT),
        name="denoised_band",
    )(place, *quarters, start, samples)


def restore_kernel(message_ref, out_ref):
    bands, _, total = out_ref.shape
    sources, _, width = message_ref.shape
    part = width - 128
    for i in range(sources):
        unit = off_lanes(message_ref[i, 0:1, part:])
        b, first = divmod(i * part, total)
        out_ref[b, :, first : first + part] = unsquared(message_ref[i, :, :part]) * unit


def restored(message, bands):
    sources, own, width = message.shape
    total = sources // bands * (width - 128)
    steps = 2
    return pl.pallas_call(
        restore_kernel,
        grid=(steps,),
        in_specs=[pl.BlockSpec((sources // steps, own, width), lambda b: (b, 0, 0))],
        out_specs=pl.BlockSpec((bands // steps, own, total), lambda b: (b, 0, 0)),
        out_shape=jax.ShapeDtypeStruct((bands, own, total), jnp.float32),
        compiler_params=pltpu.CompilerParams(vmem_limit_bytes=VMEM_LIMIT),
        name="restored",
    )(message)


def shards(raw_strain, fir_taps, start_basis):
    own, samples = raw_strain.shape
    bands = fir_taps.shape[0]
    chan_count, tm_count = lax.axis_size("chan"), lax.axis_size("tm")
    place, core = lax.axis_index("chan"), lax.axis_index("tm") % 2
    half = place % 2
    rim_piece = raw_strain[:, samples - RIM :]
    before = lax.ppermute(rim_piece, "tm", [(i, i + 1) for i in range(tm_count - 1)])
    table = filter_table(fir_taps)

    message = filtered(raw_strain, before, table, chan_count).astype(SENT)
    message = lax.all_to_all(message, "chan", 0, 0, tiled=True).astype(jnp.float32)
    kept, sent, decimated = band_gram(core, message)

    pair = (kept + swapped(sent, "tm", 1)).reshape(2, 80, 128)
    sent = swapped(lax.dynamic_index_in_dim(pair, 1 - half, 0, False), "chan", 1)
    quarter = lax.dynamic_index_in_dim(pair, half, 0, False) + sent
    quarter = quarter + swapped(quarter, "tm", 2)
    others = [swapped(quarter, "tm", distance) for distance in (8, 4, 12)]
    quarter = (quarter + others[0]) + (others[1] + others[2])

    everyone = range(chan_count * tm_count)
    across = [(i, i ^ (tm_count + 1)) for i in everyone]
    four = (
        quarter,
        swapped(quarter, "tm", 1),
        swapped(quarter, "chan", 1),
        lax.ppermute(quarter, ("chan", "tm"), across),
    )
    start = lax.dynamic_index_in_dim(start_basis, place // 2, 0, False)
    result = denoised_band(jnp.stack([core, half]), four, start, decimated)

    result = result.reshape(chan_count, own, -1).astype(SENT)
    result = lax.all_to_all(result, "chan", 0, 0, tiled=True)
    return restored(result.astype(jnp.float32), bands)


def solution(mesh):
    placed = (P("chan", "tm"), P(), P())
    return jax.shard_map(
        shards, mesh=mesh, in_specs=placed, out_specs=P(None, "chan", "tm"), check_vma=False
    )
```

```python
import jax
import jax.numpy as jnp
from jax import lax
from jax.experimental import pallas as pl
from jax.experimental.pallas import tpu as pltpu
from jax.sharding import PartitionSpec as P

ITERS = 3
RIM = 128
STEP = 512
WINDOW = STEP + RIM
HIGHEST = lax.Precision.HIGHEST
VMEM_LIMIT = 24 * 1024 * 1024
SENT = jnp.float16
POWERS = (14,) * 9 + (8, 4, 2, 1)


def swapped(block, axis, distance):
    route = [(i, i ^ distance) for i in range(lax.axis_size(axis))]
    return lax.ppermute(block, axis, route)


def dot_nt(a, b, precision=None):
    return lax.dot_general(
        a, b, (((1,), (1,)), ((), ())), precision=precision, preferred_element_type=jnp.float32
    )


def halves(value):
    high = value.astype(jnp.bfloat16)
    return high, (value - high.astype(jnp.float32)).astype(jnp.bfloat16)


def table_kernel(taps_ref, table_ref):
    for b in range(taps_ref.shape[0]):
        row = jnp.concatenate(
            [taps_ref[b].astype(jnp.float32), jnp.zeros((1, STEP), jnp.float32)], axis=1
        )
        table = pltpu.roll(jnp.broadcast_to(row, (128, WINDOW)), 4, 1, stride=4, stride_axis=0)
        table_ref[128 * b : 128 * b + 128, :] = table.astype(table_ref.dtype)


def filter_table(fir_taps):
    return pl.pallas_call(
        table_kernel,
        out_shape=jax.ShapeDtypeStruct((128 * fir_taps.shape[0], WINDOW), fir_taps.dtype),
        compiler_params=pltpu.CompilerParams(vmem_limit_bytes=16 * 1024 * 1024),
        name="filter_table",
    )(fir_taps[:, None, :])


def powers_below(value):
    value = jnp.maximum(value, 2.0**-100)
    factors = []
    for power in POWERS:
        factor = jnp.where(
            value >= 2.0**power, 2.0**power, jnp.where(value < 2.0**-power, 2.0**-power, 1.0)
        )
        value = value / factor
        factors.append(factor)
    return factors


def product(factors):
    total = factors[0]
    for factor in factors[1:]:
        total = total * factor
    return total


def on_lanes(factors, shape):
    lanes = lax.broadcasted_iota(jnp.int32, shape, len(shape) - 1)
    result = jnp.ones(shape, jnp.float32)
    for number, factor in enumerate(factors):
        result = jnp.where(lanes == number, factor, result)
    return result


def off_lanes(row):
    return product([row[..., number : number + 1] for number in range(len(POWERS))])


def squared(value):
    return value * jnp.abs(value)


def unsquared(value):
    root = jnp.sqrt(jnp.abs(value))
    return jnp.where(value < 0, -root, root)


def filter_kernel(raw_ref, table_ref, out_ref, extended_ref):
    own, samples = raw_ref.shape
    receivers, _, part = out_ref.shape
    extended_ref[:, :RIM] = jnp.zeros((own, RIM), extended_ref.dtype)
    extended_ref[:, RIM:] = raw_ref[...]
    blocks = samples // STEP
    windows = jnp.concatenate(
        [extended_ref[:, STEP * m : STEP * m + WINDOW] for m in range(blocks)], axis=0
    )
    bands = table_ref.shape[0] // 128
    share = part // 128
    for pair in range(bands // 2):
        both = dot_nt(windows, table_ref[256 * pair : 256 * pair + 256, :])
        for b in range(2):
            for m in range(blocks):
                place = (2 * pair + b) * (receivers // bands) + m // share
                first = 128 * (m % share)
                out_ref[place, :, first : first + 128] = both[
                    m * own : (m + 1) * own, 128 * b : 128 * b + 128
                ]


def message_kernel(filtered_ref, before_ref, table_ref, out_ref):
    receivers, own, part = filtered_ref.shape
    bands = table_ref.shape[0] // 128
    shares = receivers // bands
    firsts, peaks = [], []
    for b in range(bands):
        added = dot_nt(before_ref[...], table_ref[128 * b : 128 * b + 128, :RIM])
        first = filtered_ref[shares * b, :, :128] + added
        largest = jnp.max(jnp.abs(first), axis=0, keepdims=True)
        for i in range(shares):
            rest = filtered_ref[shares * b + i, :, 0 if i else 128 :]
            rest = jnp.max(jnp.abs(rest), axis=0, keepdims=True)
            for lane in range(0, rest.shape[1], 128):
                largest = jnp.maximum(largest, rest[:, lane : lane + 128])
        firsts.append(first)
        peaks.append(jnp.max(largest, axis=1, keepdims=True))
    factors = powers_below(jnp.concatenate(peaks, axis=0) * 2.0**-6)
    scale = 1.0 / product(factors)
    for i in range(receivers):
        b = i // shares
        factor = scale[b : b + 1, :]
        out_ref[i, :, :part] = squared(filtered_ref[i] * factor)
        if i % shares == 0:
            out_ref[i, :, :128] = squared(firsts[b] * factor)
        out_ref[i, :, part:] = on_lanes([each[b : b + 1, :] for each in factors], (own, 128))


def filtered(raw_strain, before, table, receivers):
    own, samples = raw_strain.shape
    part = table.shape[0] // 128 * (samples // 4) // receivers
    alone = pl.pallas_call(
        filter_kernel,
        out_shape=jax.ShapeDtypeStruct((receivers, own, part), jnp.float32),
        scratch_shapes=[pltpu.VMEM((own, samples + RIM), raw_strain.dtype)],
        compiler_params=pltpu.CompilerParams(vmem_limit_bytes=VMEM_LIMIT),
        cost_estimate=pl.CostEstimate(
            flops=2 * 512 * 640 * 1024, bytes_accessed=4 << 20, transcendentals=0
        ),
        name="filtered",
    )(raw_strain, table)
    return pl.pallas_call(
        message_kernel,
        out_shape=jax.ShapeDtypeStruct((receivers, own, part + 128), jnp.float32),
        compiler_params=pltpu.CompilerParams(vmem_limit_bytes=VMEM_LIMIT),
        name="message",
    )(alone, before, table)


def gram_kernel(core_ref, message_ref, kept_ref, sent_ref, samples_ref, packed_ref):
    core = core_ref[0]
    count = packed_ref.shape[0] // 2
    lanes = lax.broadcasted_iota(jnp.int32, (64, 128), 1)
    sources, own, width = message_ref.shape
    for i in range(sources):
        unit = off_lanes(message_ref[i, 0:1, width - 128 :])
        samples_ref[i * own : (i + 1) * own, :] = (
            unsquared(message_ref[i, :, : width - 128]) * unit
        )
    high, low = halves(samples_ref[...])
    gram = dot_nt(high, high) + dot_nt(high, low) + dot_nt(low, high)
    packed_ref[0:64, :] = gram[0:64, 0:128]
    packed_ref[64:128, :] = gram[0:64, 128:256]
    packed_ref[128:192, :] = gram[64:128, 128:256]
    packed_ref[192:256, :] = gram[128:192, 128:256]
    last = pltpu.roll(gram[192:256, 128:256], 64, 1)
    packed_ref[256:320, :] = jnp.where(lanes < 64, last, gram[64:128, 0:128])
    kept_ref[...] = packed_ref[pl.ds(pl.multiple_of(core * count, 8), count), :]
    sent_ref[...] = packed_ref[pl.ds(pl.multiple_of((1 - core) * count, 8), count), :]


def band_gram(core, message):
    sources, own, width = message.shape
    samples = jax.ShapeDtypeStruct((sources * own, width - 128), jnp.float32)
    half = jax.ShapeDtypeStruct((160, 128), jnp.float32)
    return pl.pallas_call(
        gram_kernel,
        in_specs=[
            pl.BlockSpec(memory_space=pltpu.SMEM),
            pl.BlockSpec(memory_space=pltpu.VMEM),
        ],
        out_shape=[half, half, samples],
        scratch_shapes=[pltpu.VMEM((320, 128), jnp.float32)],
        compiler_params=pltpu.CompilerParams(vmem_limit_bytes=VMEM_LIMIT),
        name="band_gram",
    )(core.reshape(1), message)


def unpacked(packed):
    first, corner = packed[0:64], packed[256:320]
    upper = jnp.concatenate(
        [first, jnp.concatenate([first.T[64:128], corner[:, 64:128]], axis=1)], axis=0
    )
    third = packed[192:256]
    lower = jnp.concatenate(
        [third, jnp.concatenate([third.T[64:128], corner[:, 0:64]], axis=1)], axis=0
    )
    across = packed[64:192]
    return jnp.concatenate(
        [
            jnp.concatenate([upper, across], axis=1),
            jnp.concatenate([across.T, lower], axis=1),
        ],
        axis=0,
    )


def decimated_gram(core, windows, table):
    channels, samples = windows.shape
    bands = table.shape[0] // 128
    half = jax.ShapeDtypeStruct((bands, 160, 128), jnp.float32)
    half_spec = pl.BlockSpec((2, 160, 128), lambda b: (b, 0, 0))
    count = (samples - RIM) // 4
    piece = jax.ShapeDtypeStruct((bands, channels, count), jnp.bfloat16)
    piece_spec = pl.BlockSpec((2, channels, count), lambda b: (b, 0, 0))
    return pl.pallas_call(
        gram_kernel,
        grid=(bands // 2,),
        in_specs=[
            pl.BlockSpec(memory_space=pltpu.SMEM),
            pl.BlockSpec((channels, samples), lambda b: (0, 0)),
            pl.BlockSpec((256, WINDOW), lambda b: (b, 0)),
        ],
        out_specs=[half_spec, half_spec, piece_spec, piece_spec],
        out_shape=[half, half, piece, piece],
        scratch_shapes=[pltpu.VMEM((320, 128), jnp.float32)],
        compiler_params=pltpu.CompilerParams(vmem_limit_bytes=VMEM_LIMIT),
        name="decimated_gram",
    )(core.reshape(1), windows, table)


def inverse_cholesky(compact):
    rank = compact.shape[0]
    rows = lax.broadcasted_iota(jnp.int32, (rank, rank), 0)
    columns = lax.broadcasted_iota(jnp.int32, (rank, rank), 1)
    unit = (rows == columns).astype(jnp.float32)
    both = jnp.concatenate([compact, unit], axis=1)
    below = lax.broadcasted_iota(jnp.int32, both.shape, 0)
    for block in range(0, rank, 8):
        spread = [
            jnp.broadcast_to(both[:, block + p : block + p + 1], both.shape) for p in range(8)
        ]
        for p in range(8):
            j = block + p
            column = spread[p]
            factor = jnp.where(below > j, column * (1.0 / column[j : j + 1, :]), 0.0)
            both = both - factor * both[j : j + 1, :]
            for q in range(p + 1, 8):
                spread[q] = spread[q] - factor * spread[q][j : j + 1, :]
    pivots = jnp.sum(unit * both[:, :rank], axis=1, keepdims=True)
    return both[:, rank:] / jnp.sqrt(pivots)


def refine_kernel(
    place_ref, mine_ref, core_ref, chan_ref, both_ref, start_ref, samples_ref, out_ref, gram_ref
):
    core, half = place_ref[0], place_ref[1]
    near = jnp.where(core == 0, mine_ref[...], core_ref[...])
    near_next = jnp.where(core == 0, core_ref[...], mine_ref[...])
    far = jnp.where(core == 0, chan_ref[...], both_ref[...])
    far_next = jnp.where(core == 0, both_ref[...], chan_ref[...])
    packed = jnp.concatenate(
        [
            jnp.where(half == 0, near, far),
            jnp.where(half == 0, far, near),
            jnp.where(half == 0, near_next, far_next),
            jnp.where(half == 0, far_next, near_next),
        ],
        axis=0,
    )
    gram_ref[...] = unpacked(packed)
    basis = start_ref[...]
    for _ in range(ITERS):
        image = jnp.dot(gram_ref[...], basis, precision=HIGHEST, preferred_element_type=jnp.float32)
        compact = lax.dot_general(
            image,
            image,
            (((0,), (0,)), ((), ())),
            precision=HIGHEST,
            preferred_element_type=jnp.float32,
        )
        basis = dot_nt(image, inverse_cholesky(compact), HIGHEST)
    part = samples_ref.shape[1]
    peak = jnp.zeros((1, STEP), jnp.float32)
    basis_high, basis_low = halves(basis)
    left = jnp.concatenate([basis_high, basis_low, basis_high], axis=1)
    rank = basis.shape[1]
    for first in range(0, part, STEP):
        columns = slice(first, first + STEP)
        samples_high, samples_low = halves(samples_ref[:, columns])
        both = lax.dot_general(
            left[:, : 2 * rank],
            samples_high,
            (((0,), (0,)), ((), ())),
            preferred_element_type=jnp.float32,
        )
        coefficients = both[:rank] + both[rank:]
        coefficients += lax.dot_general(
            basis_high,
            samples_low,
            (((0,), (0,)), ((), ())),
            preferred_element_type=jnp.float32,
        )
        high, low = halves(coefficients)
        result = jnp.dot(
            left,
            jnp.concatenate([high, high, low], axis=0),
            preferred_element_type=jnp.float32,
        )
        out_ref[:, columns] = result
        peak = jnp.maximum(peak, jnp.max(jnp.abs(result), axis=0, keepdims=True))
    factors = powers_below(jnp.max(peak, axis=1, keepdims=True) * 2.0**-6)
    scale = 1.0 / product(factors)
    for first in range(0, part, STEP):
        columns = slice(first, first + STEP)
        out_ref[:, columns] = squared(out_ref[:, columns] * scale)
    out_ref[:, part:] = on_lanes(factors, (out_ref.shape[0], 128))


def denoised_band(place, quarters, start, samples):
    channels = start.shape[0]
    return pl.pallas_call(
        refine_kernel,
        in_specs=[pl.BlockSpec(memory_space=pltpu.SMEM)]
        + [pl.BlockSpec(memory_space=pltpu.VMEM)] * 6,
        out_specs=pl.BlockSpec(memory_space=pltpu.VMEM),
        out_shape=jax.ShapeDtypeStruct((channels, samples.shape[1] + 128), jnp.float32),
        scratch_shapes=[pltpu.VMEM((channels, channels), jnp.float32)],
        compiler_params=pltpu.CompilerParams(vmem_limit_bytes=VMEM_LIMIT),
        name="denoised_band",
    )(place, *quarters, start, samples)


def restore_kernel(message_ref, out_ref):
    bands, _, total = out_ref.shape
    sources, _, width = message_ref.shape
    part = width - 128
    for i in range(sources):
        unit = off_lanes(message_ref[i, 0:1, part:])
        b, first = divmod(i * part, total)
        out_ref[b, :, first : first + part] = unsquared(message_ref[i, :, :part]) * unit


def restored(message, bands):
    sources, own, width = message.shape
    total = sources // bands * (width - 128)
    steps = 2
    return pl.pallas_call(
        restore_kernel,
        grid=(steps,),
        in_specs=[pl.BlockSpec((sources // steps, own, width), lambda b: (b, 0, 0))],
        out_specs=pl.BlockSpec((bands // steps, own, total), lambda b: (b, 0, 0)),
        out_shape=jax.ShapeDtypeStruct((bands, own, total), jnp.float32),
        compiler_params=pltpu.CompilerParams(vmem_limit_bytes=VMEM_LIMIT),
        name="restored",
    )(message)


def shards(raw_strain, fir_taps, start_basis):
    own, samples = raw_strain.shape
    bands = fir_taps.shape[0]
    chan_count, tm_count = lax.axis_size("chan"), lax.axis_size("tm")
    place, core = lax.axis_index("chan"), lax.axis_index("tm") % 2
    half = place % 2
    rim_piece = raw_strain[:, samples - RIM :]
    before = lax.ppermute(rim_piece, "tm", [(i, i + 1) for i in range(tm_count - 1)])
    table = filter_table(fir_taps)

    message = filtered(raw_strain, before, table, chan_count).astype(SENT)
    message = lax.all_to_all(message, "chan", 0, 0, tiled=True).astype(jnp.float32)
    kept, sent, decimated = band_gram(core, message)

    pair = (kept + swapped(sent, "tm", 1)).reshape(2, 80, 128)
    sent = swapped(lax.dynamic_index_in_dim(pair, 1 - half, 0, False), "chan", 1)
    quarter = lax.dynamic_index_in_dim(pair, half, 0, False) + sent
    quarter = quarter + swapped(quarter, "tm", 2)
    others = [swapped(quarter, "tm", distance) for distance in (8, 4, 12)]
    quarter = (quarter + others[0]) + (others[1] + others[2])

    everyone = range(chan_count * tm_count)
    across = [(i, i ^ (tm_count + 1)) for i in everyone]
    four = (
        quarter,
        swapped(quarter, "tm", 1),
        swapped(quarter, "chan", 1),
        lax.ppermute(quarter, ("chan", "tm"), across),
    )
    start = lax.dynamic_index_in_dim(start_basis, place // 2, 0, False)
    result = denoised_band(jnp.stack([core, half]), four, start, decimated)

    result = result.reshape(chan_count, own, -1).astype(SENT)
    result = lax.all_to_all(result, "chan", 0, 0, tiled=True)
    return restored(result.astype(jnp.float32), bands)


def solution(mesh):
    placed = (P("chan", "tm"), P(), P())
    return jax.shard_map(
        shards, mesh=mesh, in_specs=placed, out_specs=P(None, "chan", "tm"), check_vma=False
    )
```

```python
import jax
import jax.numpy as jnp
from jax import lax
from jax.experimental import pallas as pl
from jax.experimental.pallas import tpu as pltpu
from jax.sharding import PartitionSpec as P

ITERS = 3
RIM = 128
STEP = 512
WINDOW = STEP + RIM
HIGHEST = lax.Precision.HIGHEST
VMEM_LIMIT = 24 * 1024 * 1024
SENT = jnp.float16
POWERS = (14,) * 9 + (8, 4, 2, 1)


def swapped(block, axis, distance):
    route = [(i, i ^ distance) for i in range(lax.axis_size(axis))]
    return lax.ppermute(block, axis, route)


def dot_nt(a, b, precision=None):
    return lax.dot_general(
        a, b, (((1,), (1,)), ((), ())), precision=precision, preferred_element_type=jnp.float32
    )


def halves(value):
    high = value.astype(jnp.bfloat16)
    return high, (value - high.astype(jnp.float32)).astype(jnp.bfloat16)


def table_kernel(taps_ref, table_ref):
    for b in range(taps_ref.shape[0]):
        row = jnp.concatenate(
            [taps_ref[b].astype(jnp.float32), jnp.zeros((1, STEP), jnp.float32)], axis=1
        )
        table = pltpu.roll(jnp.broadcast_to(row, (128, WINDOW)), 4, 1, stride=4, stride_axis=0)
        table_ref[128 * b : 128 * b + 128, :] = table.astype(table_ref.dtype)


def filter_table(fir_taps):
    return pl.pallas_call(
        table_kernel,
        out_shape=jax.ShapeDtypeStruct((128 * fir_taps.shape[0], WINDOW), fir_taps.dtype),
        compiler_params=pltpu.CompilerParams(vmem_limit_bytes=16 * 1024 * 1024),
        name="filter_table",
    )(fir_taps[:, None, :])


def powers_below(value):
    value = jnp.maximum(value, 2.0**-100)
    factors = []
    for power in POWERS:
        factor = jnp.where(
            value >= 2.0**power, 2.0**power, jnp.where(value < 2.0**-power, 2.0**-power, 1.0)
        )
        value = value / factor
        factors.append(factor)
    return factors


def product(factors):
    total = factors[0]
    for factor in factors[1:]:
        total = total * factor
    return total


def on_lanes(factors, shape):
    lanes = lax.broadcasted_iota(jnp.int32, shape, len(shape) - 1)
    result = jnp.ones(shape, jnp.float32)
    for number, factor in enumerate(factors):
        result = jnp.where(lanes == number, factor, result)
    return result


def off_lanes(row):
    return product([row[..., number : number + 1] for number in range(len(POWERS))])


def squared(value):
    return value * jnp.abs(value)


def unsquared(value):
    root = jnp.sqrt(jnp.abs(value))
    return jnp.where(value < 0, -root, root)


def filter_kernel(raw_ref, before_ref, table_ref, out_ref, extended_ref):
    own, samples = raw_ref.shape
    receivers, _, width = out_ref.shape
    part = width - 128
    extended_ref[:, :RIM] = before_ref[...]
    extended_ref[:, RIM:] = raw_ref[...]
    blocks = samples // STEP
    windows = jnp.concatenate(
        [extended_ref[:, STEP * m : STEP * m + WINDOW] for m in range(blocks)], axis=0
    )
    bands = table_ref.shape[0] // 128
    share = part // 128
    peaks = []
    for pair in range(bands // 2):
        both = dot_nt(windows, table_ref[256 * pair : 256 * pair + 256, :])
        for b in range(2):
            largest = jnp.max(jnp.abs(both[:, 128 * b : 128 * b + 128]), axis=0, keepdims=True)
            peaks.append(jnp.max(largest, axis=1, keepdims=True))
            for m in range(blocks):
                place = (2 * pair + b) * (receivers // bands) + m // share
                first = 128 * (m % share)
                out_ref[place, :, first : first + 128] = both[
                    m * own : (m + 1) * own, 128 * b : 128 * b + 128
                ]
    factors = powers_below(jnp.concatenate(peaks, axis=0) * 2.0**-6)
    scale = 1.0 / product(factors)
    for i in range(receivers):
        b = i // (receivers // bands)
        out_ref[i, :, :part] = squared(out_ref[i, :, :part] * scale[b : b + 1, :])
        out_ref[i, :, part:] = on_lanes([factor[b : b + 1, :] for factor in factors], (own, 128))


def filtered(raw_strain, before, table, receivers):
    own, samples = raw_strain.shape
    part = table.shape[0] // 128 * (samples // 4) // receivers
    return pl.pallas_call(
        filter_kernel,
        out_shape=jax.ShapeDtypeStruct((receivers, own, part + 128), jnp.float32),
        scratch_shapes=[pltpu.VMEM((own, samples + RIM), raw_strain.dtype)],
        compiler_params=pltpu.CompilerParams(vmem_limit_bytes=VMEM_LIMIT),
        name="filtered",
    )(raw_strain, before, table)


def gram_kernel(core_ref, message_ref, kept_ref, sent_ref, samples_ref, packed_ref):
    core = core_ref[0]
    count = packed_ref.shape[0] // 2
    lanes = lax.broadcasted_iota(jnp.int32, (64, 128), 1)
    sources, own, width = message_ref.shape
    for i in range(sources):
        unit = off_lanes(message_ref[i, 0:1, width - 128 :])
        samples_ref[i * own : (i + 1) * own, :] = (
            unsquared(message_ref[i, :, : width - 128]) * unit
        )
    high, low = halves(samples_ref[...])
    gram = dot_nt(high, high) + dot_nt(high, low) + dot_nt(low, high)
    packed_ref[0:64, :] = gram[0:64, 0:128]
    packed_ref[64:128, :] = gram[0:64, 128:256]
    packed_ref[128:192, :] = gram[64:128, 128:256]
    packed_ref[192:256, :] = gram[128:192, 128:256]
    last = pltpu.roll(gram[192:256, 128:256], 64, 1)
    packed_ref[256:320, :] = jnp.where(lanes < 64, last, gram[64:128, 0:128])
    kept_ref[...] = packed_ref[pl.ds(pl.multiple_of(core * count, 8), count), :]
    sent_ref[...] = packed_ref[pl.ds(pl.multiple_of((1 - core) * count, 8), count), :]


def band_gram(core, message):
    sources, own, width = message.shape
    samples = jax.ShapeDtypeStruct((sources * own, width - 128), jnp.float32)
    half = jax.ShapeDtypeStruct((160, 128), jnp.float32)
    return pl.pallas_call(
        gram_kernel,
        in_specs=[
            pl.BlockSpec(memory_space=pltpu.SMEM),
            pl.BlockSpec(memory_space=pltpu.VMEM),
        ],
        out_shape=[half, half, samples],
        scratch_shapes=[pltpu.VMEM((320, 128), jnp.float32)],
        compiler_params=pltpu.CompilerParams(vmem_limit_bytes=VMEM_LIMIT),
        name="band_gram",
    )(core.reshape(1), message)


def unpacked(packed):
    first, corner = packed[0:64], packed[256:320]
    upper = jnp.concatenate(
        [first, jnp.concatenate([first.T[64:128], corner[:, 64:128]], axis=1)], axis=0
    )
    third = packed[192:256]
    lower = jnp.concatenate(
        [third, jnp.concatenate([third.T[64:128], corner[:, 0:64]], axis=1)], axis=0
    )
    across = packed[64:192]
    return jnp.concatenate(
        [
            jnp.concatenate([upper, across], axis=1),
            jnp.concatenate([across.T, lower], axis=1),
        ],
        axis=0,
    )


def decimated_gram(core, windows, table):
    channels, samples = windows.shape
    bands = table.shape[0] // 128
    half = jax.ShapeDtypeStruct((bands, 160, 128), jnp.float32)
    half_spec = pl.BlockSpec((2, 160, 128), lambda b: (b, 0, 0))
    count = (samples - RIM) // 4
    piece = jax.ShapeDtypeStruct((bands, channels, count), jnp.bfloat16)
    piece_spec = pl.BlockSpec((2, channels, count), lambda b: (b, 0, 0))
    return pl.pallas_call(
        gram_kernel,
        grid=(bands // 2,),
        in_specs=[
            pl.BlockSpec(memory_space=pltpu.SMEM),
            pl.BlockSpec((channels, samples), lambda b: (0, 0)),
            pl.BlockSpec((256, WINDOW), lambda b: (b, 0)),
        ],
        out_specs=[half_spec, half_spec, piece_spec, piece_spec],
        out_shape=[half, half, piece, piece],
        scratch_shapes=[pltpu.VMEM((320, 128), jnp.float32)],
        compiler_params=pltpu.CompilerParams(vmem_limit_bytes=VMEM_LIMIT),
        name="decimated_gram",
    )(core.reshape(1), windows, table)


def inverse_cholesky(compact):
    rank = compact.shape[0]
    rows = lax.broadcasted_iota(jnp.int32, (rank, rank), 0)
    columns = lax.broadcasted_iota(jnp.int32, (rank, rank), 1)
    unit = (rows == columns).astype(jnp.float32)
    both = jnp.concatenate([compact, unit], axis=1)
    below = lax.broadcasted_iota(jnp.int32, both.shape, 0)
    for block in range(0, rank, 16):
        spread = [
            jnp.broadcast_to(both[:, block + p : block + p + 1], both.shape) for p in range(16)
        ]
        for p in range(16):
            j = block + p
            column = spread[p]
            factor = jnp.where(below > j, column * (1.0 / column[j : j + 1, :]), 0.0)
            both = both - factor * both[j : j + 1, :]
            for q in range(p + 1, 16):
                spread[q] = spread[q] - factor * spread[q][j : j + 1, :]
    pivots = jnp.sum(unit * both[:, :rank], axis=1, keepdims=True)
    return both[:, rank:] / jnp.sqrt(pivots)


def refine_kernel(
    place_ref, mine_ref, core_ref, chan_ref, both_ref, start_ref, samples_ref, out_ref, gram_ref
):
    core, half = place_ref[0], place_ref[1]
    near = jnp.where(core == 0, mine_ref[...], core_ref[...])
    near_next = jnp.where(core == 0, core_ref[...], mine_ref[...])
    far = jnp.where(core == 0, chan_ref[...], both_ref[...])
    far_next = jnp.where(core == 0, both_ref[...], chan_ref[...])
    packed = jnp.concatenate(
        [
            jnp.where(half == 0, near, far),
            jnp.where(half == 0, far, near),
            jnp.where(half == 0, near_next, far_next),
            jnp.where(half == 0, far_next, near_next),
        ],
        axis=0,
    )
    gram_ref[...] = unpacked(packed)
    basis = start_ref[...]
    for _ in range(ITERS):
        image = jnp.dot(gram_ref[...], basis, precision=HIGHEST, preferred_element_type=jnp.float32)
        compact = lax.dot_general(
            image,
            image,
            (((0,), (0,)), ((), ())),
            precision=HIGHEST,
            preferred_element_type=jnp.float32,
        )
        basis = dot_nt(image, inverse_cholesky(compact), HIGHEST)
    part = samples_ref.shape[1]
    peak = jnp.zeros((1, STEP), jnp.float32)
    basis_high, basis_low = halves(basis)
    left = jnp.concatenate([basis_high, basis_low, basis_high], axis=1)
    rank = basis.shape[1]
    for first in range(0, part, STEP):
        columns = slice(first, first + STEP)
        samples_high, samples_low = halves(samples_ref[:, columns])
        both = lax.dot_general(
            left[:, : 2 * rank],
            samples_high,
            (((0,), (0,)), ((), ())),
            preferred_element_type=jnp.float32,
        )
        coefficients = both[:rank] + both[rank:]
        coefficients += lax.dot_general(
            basis_high,
            samples_low,
            (((0,), (0,)), ((), ())),
            preferred_element_type=jnp.float32,
        )
        high, low = halves(coefficients)
        result = jnp.dot(
            left,
            jnp.concatenate([high, high, low], axis=0),
            preferred_element_type=jnp.float32,
        )
        out_ref[:, columns] = result
        peak = jnp.maximum(peak, jnp.max(jnp.abs(result), axis=0, keepdims=True))
    factors = powers_below(jnp.max(peak, axis=1, keepdims=True) * 2.0**-6)
    scale = 1.0 / product(factors)
    for first in range(0, part, STEP):
        columns = slice(first, first + STEP)
        out_ref[:, columns] = squared(out_ref[:, columns] * scale)
    out_ref[:, part:] = on_lanes(factors, (out_ref.shape[0], 128))


def denoised_band(place, quarters, start, samples):
    channels = start.shape[0]
    return pl.pallas_call(
        refine_kernel,
        in_specs=[pl.BlockSpec(memory_space=pltpu.SMEM)]
        + [pl.BlockSpec(memory_space=pltpu.VMEM)] * 6,
        out_specs=pl.BlockSpec(memory_space=pltpu.VMEM),
        out_shape=jax.ShapeDtypeStruct((channels, samples.shape[1] + 128), jnp.float32),
        scratch_shapes=[pltpu.VMEM((channels, channels), jnp.float32)],
        compiler_params=pltpu.CompilerParams(vmem_limit_bytes=VMEM_LIMIT),
        name="denoised_band",
    )(place, *quarters, start, samples)


def restore_kernel(message_ref, out_ref):
    bands, _, total = out_ref.shape
    sources, _, width = message_ref.shape
    part = width - 128
    for i in range(sources):
        unit = off_lanes(message_ref[i, 0:1, part:])
        b, first = divmod(i * part, total)
        out_ref[b, :, first : first + part] = unsquared(message_ref[i, :, :part]) * unit


def restored(message, bands):
    sources, own, width = message.shape
    total = sources // bands * (width - 128)
    steps = 2
    return pl.pallas_call(
        restore_kernel,
        grid=(steps,),
        in_specs=[pl.BlockSpec((sources // steps, own, width), lambda b: (b, 0, 0))],
        out_specs=pl.BlockSpec((bands // steps, own, total), lambda b: (b, 0, 0)),
        out_shape=jax.ShapeDtypeStruct((bands, own, total), jnp.float32),
        compiler_params=pltpu.CompilerParams(vmem_limit_bytes=VMEM_LIMIT),
        name="restored",
    )(message)


def shards(raw_strain, fir_taps, start_basis):
    own, samples = raw_strain.shape
    bands = fir_taps.shape[0]
    chan_count, tm_count = lax.axis_size("chan"), lax.axis_size("tm")
    place, core = lax.axis_index("chan"), lax.axis_index("tm") % 2
    half = place % 2
    rim_piece = raw_strain[:, samples - RIM :]
    before = lax.ppermute(rim_piece, "tm", [(i, i + 1) for i in range(tm_count - 1)])
    table = filter_table(fir_taps)

    message = filtered(raw_strain, before, table, chan_count).astype(SENT)
    message = lax.all_to_all(message, "chan", 0, 0, tiled=True).astype(jnp.float32)
    kept, sent, decimated = band_gram(core, message)

    pair = (kept + swapped(sent, "tm", 1)).reshape(2, 80, 128)
    sent = swapped(lax.dynamic_index_in_dim(pair, 1 - half, 0, False), "chan", 1)
    quarter = lax.dynamic_index_in_dim(pair, half, 0, False) + sent
    quarter = quarter + swapped(quarter, "tm", 2)
    others = [swapped(quarter, "tm", distance) for distance in (8, 4, 12)]
    quarter = (quarter + others[0]) + (others[1] + others[2])

    everyone = range(chan_count * tm_count)
    across = [(i, i ^ (tm_count + 1)) for i in everyone]
    four = (
        quarter,
        swapped(quarter, "tm", 1),
        swapped(quarter, "chan", 1),
        lax.ppermute(quarter, ("chan", "tm"), across),
    )
    start = lax.dynamic_index_in_dim(start_basis, place // 2, 0, False)
    result = denoised_band(jnp.stack([core, half]), four, start, decimated)

    result = result.reshape(chan_count, own, -1).astype(SENT)
    result = lax.all_to_all(result, "chan", 0, 0, tiled=True)
    return restored(result.astype(jnp.float32), bands)


def solution(mesh):
    placed = (P("chan", "tm"), P(), P())
    return jax.shard_map(
        shards, mesh=mesh, in_specs=placed, out_specs=P(None, "chan", "tm"), check_vma=False
    )
```

```python
import jax
import jax.numpy as jnp
from jax import lax
from jax.experimental import pallas as pl
from jax.experimental.pallas import tpu as pltpu
from jax.sharding import PartitionSpec as P

ITERS = 3
RIM = 128
STEP = 512
WINDOW = STEP + RIM
HIGHEST = lax.Precision.HIGHEST
VMEM_LIMIT = 24 * 1024 * 1024
SENT = jnp.float16
POWERS = (14,) * 9 + (8, 4, 2, 1)


def swapped(block, axis, distance):
    route = [(i, i ^ distance) for i in range(lax.axis_size(axis))]
    return lax.ppermute(block, axis, route)


def dot_nt(a, b, precision=None):
    return lax.dot_general(
        a, b, (((1,), (1,)), ((), ())), precision=precision, preferred_element_type=jnp.float32
    )


def halves(value):
    high = value.astype(jnp.bfloat16)
    return high, (value - high.astype(jnp.float32)).astype(jnp.bfloat16)


def table_kernel(taps_ref, table_ref):
    for b in range(taps_ref.shape[0]):
        row = jnp.concatenate(
            [taps_ref[b].astype(jnp.float32), jnp.zeros((1, STEP), jnp.float32)], axis=1
        )
        table = pltpu.roll(jnp.broadcast_to(row, (128, WINDOW)), 4, 1, stride=4, stride_axis=0)
        table_ref[128 * b : 128 * b + 128, :] = table.astype(table_ref.dtype)


def filter_table(fir_taps):
    return pl.pallas_call(
        table_kernel,
        out_shape=jax.ShapeDtypeStruct((128 * fir_taps.shape[0], WINDOW), fir_taps.dtype),
        compiler_params=pltpu.CompilerParams(vmem_limit_bytes=16 * 1024 * 1024),
        name="filter_table",
    )(fir_taps[:, None, :])


def powers_below(value):
    value = jnp.maximum(value, 2.0**-100)
    factors = []
    for power in POWERS:
        factor = jnp.where(
            value >= 2.0**power, 2.0**power, jnp.where(value < 2.0**-power, 2.0**-power, 1.0)
        )
        value = value / factor
        factors.append(factor)
    return factors


def product(factors):
    total = factors[0]
    for factor in factors[1:]:
        total = total * factor
    return total


def on_lanes(factors, shape):
    lanes = lax.broadcasted_iota(jnp.int32, shape, len(shape) - 1)
    result = jnp.ones(shape, jnp.float32)
    for number, factor in enumerate(factors):
        result = jnp.where(lanes == number, factor, result)
    return result


def off_lanes(row):
    return product([row[..., number : number + 1] for number in range(len(POWERS))])


def squared(value):
    return value * jnp.abs(value)


def unsquared(value):
    root = jnp.sqrt(jnp.abs(value))
    return jnp.where(value < 0, -root, root)


def filter_kernel(raw_ref, before_ref, table_ref, out_ref, extended_ref):
    own, samples = raw_ref.shape
    receivers, _, width = out_ref.shape
    part = width - 128
    extended_ref[:, :RIM] = before_ref[...]
    extended_ref[:, RIM:] = raw_ref[...]
    blocks = samples // STEP
    windows = jnp.concatenate(
        [extended_ref[:, STEP * m : STEP * m + WINDOW] for m in range(blocks)], axis=0
    )
    bands = table_ref.shape[0] // 128
    share = part // 128
    peaks = []
    for pair in range(bands // 2):
        both = dot_nt(windows, table_ref[256 * pair : 256 * pair + 256, :])
        for b in range(2):
            largest = jnp.max(jnp.abs(both[:, 128 * b : 128 * b + 128]), axis=0, keepdims=True)
            peaks.append(jnp.max(largest, axis=1, keepdims=True))
            for m in range(blocks):
                place = (2 * pair + b) * (receivers // bands) + m // share
                first = 128 * (m % share)
                out_ref[place, :, first : first + 128] = both[
                    m * own : (m + 1) * own, 128 * b : 128 * b + 128
                ]
    factors = powers_below(jnp.concatenate(peaks, axis=0) * 2.0**-6)
    scale = 1.0 / product(factors)
    for i in range(receivers):
        b = i // (receivers // bands)
        out_ref[i, :, :part] = squared(out_ref[i, :, :part] * scale[b : b + 1, :])
        out_ref[i, :, part:] = on_lanes([factor[b : b + 1, :] for factor in factors], (own, 128))


def filtered(raw_strain, before, table, receivers):
    own, samples = raw_strain.shape
    part = table.shape[0] // 128 * (samples // 4) // receivers
    return pl.pallas_call(
        filter_kernel,
        out_shape=jax.ShapeDtypeStruct((receivers, own, part + 128), jnp.float32),
        scratch_shapes=[pltpu.VMEM((own, samples + RIM), raw_strain.dtype)],
        compiler_params=pltpu.CompilerParams(vmem_limit_bytes=VMEM_LIMIT),
        name="filtered",
    )(raw_strain, before, table)


def gram_kernel(core_ref, message_ref, kept_ref, sent_ref, samples_ref, packed_ref):
    core = core_ref[0]
    count = packed_ref.shape[0] // 2
    lanes = lax.broadcasted_iota(jnp.int32, (64, 128), 1)
    sources, own, width = message_ref.shape
    for i in range(sources):
        unit = off_lanes(message_ref[i, 0:1, width - 128 :])
        samples_ref[i * own : (i + 1) * own, :] = (
            unsquared(message_ref[i, :, : width - 128]) * unit
        )
    high, low = halves(samples_ref[...])
    gram = dot_nt(high, high) + dot_nt(high, low) + dot_nt(low, high)
    packed_ref[0:64, :] = gram[0:64, 0:128]
    packed_ref[64:128, :] = gram[0:64, 128:256]
    packed_ref[128:192, :] = gram[64:128, 128:256]
    packed_ref[192:256, :] = gram[128:192, 128:256]
    last = pltpu.roll(gram[192:256, 128:256], 64, 1)
    packed_ref[256:320, :] = jnp.where(lanes < 64, last, gram[64:128, 0:128])
    kept_ref[...] = packed_ref[pl.ds(pl.multiple_of(core * count, 8), count), :]
    sent_ref[...] = packed_ref[pl.ds(pl.multiple_of((1 - core) * count, 8), count), :]


def band_gram(core, message):
    sources, own, width = message.shape
    samples = jax.ShapeDtypeStruct((sources * own, width - 128), jnp.float32)
    half = jax.ShapeDtypeStruct((160, 128), jnp.float32)
    return pl.pallas_call(
        gram_kernel,
        in_specs=[
            pl.BlockSpec(memory_space=pltpu.SMEM),
            pl.BlockSpec(memory_space=pltpu.VMEM),
        ],
        out_shape=[half, half, samples],
        scratch_shapes=[pltpu.VMEM((320, 128), jnp.float32)],
        compiler_params=pltpu.CompilerParams(vmem_limit_bytes=VMEM_LIMIT),
        name="band_gram",
    )(core.reshape(1), message)


def unpacked(packed):
    first, corner = packed[0:64], packed[256:320]
    upper = jnp.concatenate(
        [first, jnp.concatenate([first.T[64:128], corner[:, 64:128]], axis=1)], axis=0
    )
    third = packed[192:256]
    lower = jnp.concatenate(
        [third, jnp.concatenate([third.T[64:128], corner[:, 0:64]], axis=1)], axis=0
    )
    across = packed[64:192]
    return jnp.concatenate(
        [
            jnp.concatenate([upper, across], axis=1),
            jnp.concatenate([across.T, lower], axis=1),
        ],
        axis=0,
    )


def decimated_gram(core, windows, table):
    channels, samples = windows.shape
    bands = table.shape[0] // 128
    half = jax.ShapeDtypeStruct((bands, 160, 128), jnp.float32)
    half_spec = pl.BlockSpec((2, 160, 128), lambda b: (b, 0, 0))
    count = (samples - RIM) // 4
    piece = jax.ShapeDtypeStruct((bands, channels, count), jnp.bfloat16)
    piece_spec = pl.BlockSpec((2, channels, count), lambda b: (b, 0, 0))
    return pl.pallas_call(
        gram_kernel,
        grid=(bands // 2,),
        in_specs=[
            pl.BlockSpec(memory_space=pltpu.SMEM),
            pl.BlockSpec((channels, samples), lambda b: (0, 0)),
            pl.BlockSpec((256, WINDOW), lambda b: (b, 0)),
        ],
        out_specs=[half_spec, half_spec, piece_spec, piece_spec],
        out_shape=[half, half, piece, piece],
        scratch_shapes=[pltpu.VMEM((320, 128), jnp.float32)],
        compiler_params=pltpu.CompilerParams(vmem_limit_bytes=VMEM_LIMIT),
        name="decimated_gram",
    )(core.reshape(1), windows, table)


def inverse_cholesky(compact):
    rank = compact.shape[0]
    rows = lax.broadcasted_iota(jnp.int32, (rank, rank), 0)
    columns = lax.broadcasted_iota(jnp.int32, (rank, rank), 1)
    unit = (rows == columns).astype(jnp.float32)
    both = jnp.concatenate([compact, unit], axis=1)
    below = lax.broadcasted_iota(jnp.int32, both.shape, 0)
    for block in range(0, rank, 8):
        spread = [
            jnp.broadcast_to(both[:, block + p : block + p + 1], both.shape) for p in range(8)
        ]
        for p in range(8):
            j = block + p
            column = spread[p]
            factor = jnp.where(below > j, column * (1.0 / column[j : j + 1, :]), 0.0)
            both = both - factor * both[j : j + 1, :]
            for q in range(p + 1, 8):
                spread[q] = spread[q] - factor * spread[q][j : j + 1, :]
    pivots = jnp.sum(unit * both[:, :rank], axis=1, keepdims=True)
    return both[:, rank:] / jnp.sqrt(pivots)


def refine_kernel(
    place_ref, mine_ref, core_ref, chan_ref, both_ref, start_ref, samples_ref, out_ref, gram_ref
):
    core, half = place_ref[0], place_ref[1]
    near = jnp.where(core == 0, mine_ref[...], core_ref[...])
    near_next = jnp.where(core == 0, core_ref[...], mine_ref[...])
    far = jnp.where(core == 0, chan_ref[...], both_ref[...])
    far_next = jnp.where(core == 0, both_ref[...], chan_ref[...])
    packed = jnp.concatenate(
        [
            jnp.where(half == 0, near, far),
            jnp.where(half == 0, far, near),
            jnp.where(half == 0, near_next, far_next),
            jnp.where(half == 0, far_next, near_next),
        ],
        axis=0,
    )
    gram_ref[...] = unpacked(packed)
    basis = start_ref[...]
    for _ in range(ITERS):
        image = jnp.dot(gram_ref[...], basis, precision=HIGHEST, preferred_element_type=jnp.float32)
        compact = lax.dot_general(
            image,
            image,
            (((0,), (0,)), ((), ())),
            precision=HIGHEST,
            preferred_element_type=jnp.float32,
        )
        basis = dot_nt(image, inverse_cholesky(compact), HIGHEST)
    part = samples_ref.shape[1]
    peak = jnp.zeros((1, STEP), jnp.float32)
    basis_high, basis_low = halves(basis)
    left = jnp.concatenate([basis_high, basis_low, basis_high], axis=1)
    rank = basis.shape[1]
    for first in range(0, part, STEP):
        columns = slice(first, first + STEP)
        samples_high, samples_low = halves(samples_ref[:, columns])
        both = lax.dot_general(
            left[:, : 2 * rank],
            samples_high,
            (((0,), (0,)), ((), ())),
            preferred_element_type=jnp.float32,
        )
        coefficients = both[:rank] + both[rank:]
        coefficients += lax.dot_general(
            basis_high,
            samples_low,
            (((0,), (0,)), ((), ())),
            preferred_element_type=jnp.float32,
        )
        high, low = halves(coefficients)
        result = jnp.dot(
            left,
            jnp.concatenate([high, high, low], axis=0),
            preferred_element_type=jnp.float32,
        )
        out_ref[:, columns] = result
        peak = jnp.maximum(peak, jnp.max(jnp.abs(result), axis=0, keepdims=True))
    factors = powers_below(jnp.max(peak, axis=1, keepdims=True) * 2.0**-6)
    scale = 1.0 / product(factors)
    for first in range(0, part, STEP):
        columns = slice(first, first + STEP)
        out_ref[:, columns] = squared(out_ref[:, columns] * scale)
    out_ref[:, part:] = on_lanes(factors, (out_ref.shape[0], 128))


def denoised_band(place, quarters, start, samples):
    channels = start.shape[0]
    return pl.pallas_call(
        refine_kernel,
        in_specs=[pl.BlockSpec(memory_space=pltpu.SMEM)]
        + [pl.BlockSpec(memory_space=pltpu.VMEM)] * 6,
        out_specs=pl.BlockSpec(memory_space=pltpu.VMEM),
        out_shape=jax.ShapeDtypeStruct((channels, samples.shape[1] + 128), jnp.float32),
        scratch_shapes=[pltpu.VMEM((channels, channels), jnp.float32)],
        compiler_params=pltpu.CompilerParams(vmem_limit_bytes=VMEM_LIMIT),
        name="denoised_band",
    )(place, *quarters, start, samples)


def restore_kernel(message_ref, out_ref):
    bands, _, total = out_ref.shape
    sources, _, width = message_ref.shape
    part = width - 128
    for i in range(sources):
        unit = off_lanes(message_ref[i, 0:1, part:])
        b, first = divmod(i * part, total)
        out_ref[b, :, first : first + part] = unsquared(message_ref[i, :, :part]) * unit


def restored(message, bands):
    sources, own, width = message.shape
    total = sources // bands * (width - 128)
    steps = 2
    return pl.pallas_call(
        restore_kernel,
        grid=(steps,),
        in_specs=[pl.BlockSpec((sources // steps, own, width), lambda b: (b, 0, 0))],
        out_specs=pl.BlockSpec((bands // steps, own, total), lambda b: (b, 0, 0)),
        out_shape=jax.ShapeDtypeStruct((bands, own, total), jnp.float32),
        compiler_params=pltpu.CompilerParams(vmem_limit_bytes=VMEM_LIMIT),
        name="restored",
    )(message)


def shards(raw_strain, fir_taps, start_basis):
    own, samples = raw_strain.shape
    bands = fir_taps.shape[0]
    chan_count, tm_count = lax.axis_size("chan"), lax.axis_size("tm")
    place, core = lax.axis_index("chan"), lax.axis_index("tm") % 2
    half = place % 2
    rim_piece = raw_strain[:, samples - RIM :]
    before = lax.ppermute(rim_piece, "tm", [(i, i + 1) for i in range(tm_count - 1)])
    table = filter_table(fir_taps)

    message = filtered(raw_strain, before, table, chan_count).astype(SENT)
    message = lax.all_to_all(message, "chan", 0, 0, tiled=True).astype(jnp.float32)
    kept, sent, decimated = band_gram(core, message)

    pair = (kept + swapped(sent, "tm", 1)).reshape(2, 80, 128)
    sent = swapped(lax.dynamic_index_in_dim(pair, 1 - half, 0, False), "chan", 1)
    quarter = lax.dynamic_index_in_dim(pair, half, 0, False) + sent
    quarter = quarter + swapped(quarter, "tm", 2)
    others = [swapped(quarter, "tm", distance) for distance in (8, 4, 12)]
    quarter = (quarter + others[0]) + (others[1] + others[2])

    everyone = range(chan_count * tm_count)
    across = [(i, i ^ (tm_count + 1)) for i in everyone]
    both = lax.ppermute(quarter, ("chan", "tm"), across)
    beside = swapped(quarter, "chan", 1)
    four = (quarter, swapped(quarter, "tm", 1), beside, both)
    start = lax.dynamic_index_in_dim(start_basis, place // 2, 0, False)
    result = denoised_band(jnp.stack([core, half]), four, start, decimated)

    result = result.reshape(chan_count, own, -1).astype(SENT)
    result = lax.all_to_all(result, "chan", 0, 0, tiled=True)
    return restored(result.astype(jnp.float32), bands)


def solution(mesh):
    placed = (P("chan", "tm"), P(), P())
    return jax.shard_map(
        shards, mesh=mesh, in_specs=placed, out_specs=P(None, "chan", "tm"), check_vma=False
    )
```
